32 devices in a mesh: rows: 8 (over z, y), cols: 4 (over x, core).
Axes of the slice: x: 2, y: 2, z: 4, core: 2. Of those that a mesh axis runs over, the one named last changes fastest.
Arguments:
- patches: bfloat16 [192, 96, 1280], P('rows', 'cols'), may hold values from -6 to 6
- conv_taps: float32 [3, 3, 1280], replicated, may hold values from -1.5 to 1.5
- conv_bias: float32 [1280], replicated, may hold values from -3 to 3
- norm_gain: float32 [1280], replicated, may hold values from 0.1 to 1.9
- norm_bias: float32 [1280], replicated, may hold values from -3 to 3
- qkv_weight: bfloat16 [3, 1280, 1280], P(None, None, 'cols'), may hold values from -0.15625 to 0.15625
- qkv_bias: bfloat16 [3, 1280], P(None, 'cols'), may hold values from -3 to 3
Outputs:
- qkv_heads: bfloat16 [3, 16, 192, 7680], P(None, 'cols', 'rows')
The draws below stay inside these ranges and needn't reach their ends.
All inputs are finite; a program needn't handle non-finite values.
Results may differ from the reference program's by a relative error of at most 0.0047.
Values may be sent and summed in bfloat16 or wider, within the bound.
No kernel may reach another device: no remote copies, remote signals or barrier semaphores. Data moves between devices by JAX's collectives and lax.ppermute only.
A program may use at most 128 MiB of HBM per device.

```python
import jax
import jax.numpy as jnp
from jax import lax

D = 1280
HEADS = 16
HD = 80
NR = 192
NC = 96


def shard_levels(stream_key, extent, shards, least, largest):
    def one(position, shards_of):
        heights = jax.random.uniform(jax.random.fold_in(jax.random.fold_in(stream_key, 6), position), (shards_of,), jnp.float32, least / len(shards), largest / len(shards))
        return jnp.repeat(jnp.exp(heights), extent[position] // shards_of).reshape((-1,) + (1,) * (len(extent) - position - 1))

    factor_of = one(*shards[0])
    for cut in shards[1:]:
        factor_of = factor_of * one(*cut)
    return factor_of


def gaussian(stream_key, dims, width, limit, split=(), held_as=jnp.bfloat16):
    result = jax.random.normal(stream_key, dims, jnp.float32) * width
    if len(split) > 0:
        result = shard_levels(stream_key, dims, split, -0.22, 0.18) * result
    return jnp.clip(result, min=-limit, max=limit).astype(held_as)


def setup_inputs(seed: int = 0) -> dict:
    key_list = jax.random.split(jax.random.key(seed), 8)
    return {
        "patches": gaussian(key_list[0], (NR, NC, D), 1.0, 6.0, ((0, 8), (1, 4))),
        "conv_taps": gaussian(key_list[1], (3, 3, D), 0.25, 1.5, (), jnp.float32),
        "conv_bias": gaussian(key_list[2], (D,), 0.5, 3.0, (), jnp.float32),
        "norm_gain": jnp.clip(1.0 + 0.18 * jax.random.normal(key_list[3], (D,), jnp.float32), 0.1, 1.9),
        "norm_bias": gaussian(key_list[4], (D,), 0.5, 3.0, (), jnp.float32),
        "qkv_weight": gaussian(key_list[5], (3, D, D), D ** -0.5, 0.15625, ((2, 4),)),
        "qkv_bias": gaussian(key_list[6], (3, D), 0.5, 3.0, ((1, 4),)),
    }


def reference(patches, conv_taps, conv_bias, norm_gain, norm_bias, qkv_weight, qkv_bias):
    padded = jnp.pad(patches, ((1, 1), (1, 1), (0, 0)))
    mixed = patches.astype(jnp.float32) + conv_bias
    for a in range(3):
        for b in range(3):
            mixed = mixed + conv_taps[a, b] * padded[a:a + NR, b:b + NC].astype(jnp.float32)
    mean = lax.optimization_barrier(jnp.mean(mixed, axis=-1, keepdims=True))
    var = lax.optimization_barrier(jnp.mean((mixed - mean) ** 2, axis=-1, keepdims=True))
    normed = ((mixed - mean) / jnp.sqrt(var + 1e-06) * norm_gain + norm_bias).astype(jnp.bfloat16)
    flat = normed.reshape(NR * NC, D)

    def project(pair):
        weight, bias = pair
        out = jnp.dot(flat, weight, preferred_element_type=jnp.float32) + bias.astype(jnp.float32)
        out = out.astype(jnp.bfloat16).reshape(NR, NC, HEADS, HD)
        return jnp.transpose(out, (2, 0, 1, 3)).reshape(HEADS, NR, NC * HD)
    return lax.map(project, (qkv_weight, qkv_bias))
```

```python
import functools

import jax
import jax.numpy as jnp
from jax import lax
from jax.experimental import pallas as pl
from jax.experimental.pallas import tpu as pltpu
from jax.sharding import PartitionSpec as P

HD = 80
GROUP = 8
LANES = 128
EPS = 1e-06
VMEM_LIMIT = 16 * 1024 * 1024
EARLY = 4
PIECE = 96
BF16 = jnp.bfloat16
F32 = jnp.float32

VMEM = pl.BlockSpec(memory_space=pltpu.VMEM)
HBM = pl.BlockSpec(memory_space=pltpu.HBM)


def call(body, name, outs, specs, out_specs, scratch, aliases=None):
    return pl.pallas_call(
        body,
        out_shape=outs,
        in_specs=specs,
        out_specs=out_specs,
        scratch_shapes=scratch,
        input_output_aliases=aliases or {},
        compiler_params=pltpu.CompilerParams(vmem_limit_bytes=VMEM_LIMIT),
        cost_estimate=pl.CostEstimate(flops=1024, bytes_accessed=1024, transcendentals=0),
        name=name,
    )


def stencil(taps_ref, bias_ref, lanes, cells, first, count, emit):
    taps = [[taps_ref[a, pl.ds(b, 1), lanes] for b in range(3)] for a in range(3)]
    bias = bias_ref[:, lanes]
    above = here = None
    for i in range(first - 1, first + count + 1):
        l, c, r = cells(i)
        part = [taps[a][0] * l + taps[a][1] * c + taps[a][2] * r for a in range(3)]
        if i > first:
            emit(i - 1, above + part[2])
        if i >= first:
            above = here + (part[1] + c)
        here = part[0] + bias


def normalize(mixed, count, gain_ref, nbias_ref, out_ref):
    width = mixed.shape[1]
    tiles = [pl.ds(k, LANES) for k in range(0, width, LANES)]
    total = mixed[:count, tiles[0]]
    for lanes in tiles[1:]:
        total = total + mixed[:count, lanes]
    mean = jnp.sum(total, axis=1, keepdims=True) * (1.0 / width)
    square = None
    for lanes in tiles:
        centered = mixed[:count, lanes] - mean
        square = centered * centered if square is None else square + centered * centered
    scale = lax.rsqrt(jnp.sum(square, axis=1, keepdims=True) * (1.0 / width) + EPS)
    for lanes in tiles:
        value = (mixed[:count, lanes] - mean) * scale * gain_ref[:, lanes] + nbias_ref[:, lanes]
        out_ref[:count, lanes] = value.astype(BF16)


def each_tile(width, body):
    def step(k, _):
        body(pl.ds(pl.multiple_of(k * LANES, LANES), LANES))
        return 0

    lax.fori_loop(0, width // LANES, step, 0)


def middle_cells(x_ref, lanes, span):
    cols = x_ref.shape[1]

    def cells(i):
        x = x_ref[i, :, lanes].astype(F32)
        return pltpu.roll(x, 1, 0)[span], x[span], pltpu.roll(x, cols - 1, 0)[span]

    return cells


def core_of(cols_axis):
    return lax.rem(lax.axis_index(cols_axis), 2)


def first_kernel(count, x_hbm, taps_hbm, cbias_hbm, gain_hbm, nbias_hbm, out_ref, inner_ref, x_ref, taps_ref, vec_ref, mixed, *rest):
    *flat, sems = rest
    rows, cols, width = x_ref.shape
    need = count + 2
    copies = [
        pltpu.make_async_copy(x_hbm.at[pl.ds(0, need)], x_ref.at[pl.ds(0, need)], sems.at[0]),
        pltpu.make_async_copy(taps_hbm, taps_ref, sems.at[1]),
        pltpu.make_async_copy(cbias_hbm, flat[0], sems.at[2]),
        pltpu.make_async_copy(gain_hbm, flat[1], sems.at[3]),
        pltpu.make_async_copy(nbias_hbm, flat[2], sems.at[4]),
        pltpu.make_async_copy(x_hbm.at[pl.ds(need, rows - need)], x_ref.at[pl.ds(need, rows - need)], sems.at[5]),
    ]
    for copy in copies:
        copy.start()
    for copy in copies[:-1]:
        copy.wait()
    for k in range(3):
        vec_ref[k] = flat[k][...].reshape(1, width)
    span = slice(GROUP, cols - GROUP)
    wide = cols - 2 * GROUP

    def tile(lanes):
        def emit(i, value):
            mixed[pl.ds((i - 1) * wide, wide), lanes] = value

        stencil(taps_ref, vec_ref.at[0], lanes, middle_cells(x_ref, lanes, span), 1, count, emit)

    each_tile(width, tile)
    normalize(mixed, count * wide, vec_ref.at[1], vec_ref.at[2], out_ref)
    copies[-1].wait()
    core = core_of("cols")

    def sides(lanes):
        left = [x_ref[i, pl.ds(0, GROUP), lanes].astype(F32)[:1] for i in range(rows)]
        right = [x_ref[i, pl.ds(cols - GROUP, GROUP), lanes].astype(F32)[GROUP - 1 :] for i in range(rows)]
        left, right = jnp.concatenate(left, axis=0), jnp.concatenate(right, axis=0)
        out_ref[count * wide :, lanes] = jnp.where(core == 1, right, left).astype(BF16)
        inner_ref[:, lanes] = jnp.where(core == 1, left, right).astype(BF16)

    each_tile(width, sides)


def second_kernel(start, x_ref, taps_ref, vec_ref, out_ref, mixed):
    rows, cols, width = x_ref.shape
    span = slice(GROUP, cols - GROUP)
    wide = cols - 2 * GROUP
    count = rows - 1 - start

    def tile(lanes):
        def emit(i, value):
            mixed[pl.ds((i - start) * wide, wide), lanes] = value

        stencil(taps_ref, vec_ref.at[0], lanes, middle_cells(x_ref, lanes, span), start, count, emit)

    each_tile(width, tile)
    normalize(mixed, count * wide, vec_ref.at[1], vec_ref.at[2], out_ref)


def relay_kernel(beside_ref, before_ref, behind_ref, _, out_ref):
    rows = beside_ref.shape[0]
    few = before_ref.shape[0] - rows
    col, count = lax.axis_index("cols"), lax.axis_size("cols")
    core = core_of("cols")
    none = jnp.logical_or(col == 1, col == count - 2)
    out_ref[:rows, :] = beside_ref[...]
    passed = jnp.where(core == 1, before_ref[few:, :].astype(F32), behind_ref[few:, :].astype(F32))
    out_ref[rows:, :] = jnp.where(none, 0.0, passed).astype(BF16)


def halves(sides_ref, rows, lanes):
    other, passed = sides_ref[:rows, lanes].astype(F32), sides_ref[rows:, lanes].astype(F32)
    core = core_of("cols")
    return jnp.where(core == 1, other, passed), jnp.where(core == 1, passed, other)


def sides_kernel(
    x_ref, sides_ref, taps_ref, vec_ref, near_ref, far_ref, top_ref, bottom_ref, lefts, rights, mixed
):
    rows, cols, width = x_ref.shape
    place = lax.broadcasted_iota(jnp.int32, (GROUP, LANES), 0)
    inner = rows - 2
    half = inner * GROUP
    lefts[...], rights[...] = halves(sides_ref, rows, slice(None))
    for ref, at in ((top_ref, 0), (bottom_ref, rows - 1)):
        ref[:cols, :] = x_ref[at]
        ends = jnp.concatenate([lefts[at : at + 1], rights[at : at + 1]], axis=0)
        ref[cols:, :] = ends.astype(BF16)

    def tile(lanes):
        def near(i):
            x = x_ref[i, :, lanes].astype(F32)
            l = jnp.where(place == 0, lefts[pl.ds(i, 1), lanes], pltpu.roll(x, 1, 0)[:GROUP])
            return l, x[:GROUP], pltpu.roll(x, cols - 1, 0)[:GROUP]

        def far(i):
            x = x_ref[i, :, lanes].astype(F32)
            r = jnp.where(place == GROUP - 1, rights[pl.ds(i, 1), lanes], pltpu.roll(x, cols - 1, 0)[cols - GROUP :])
            return pltpu.roll(x, 1, 0)[cols - GROUP :], x[cols - GROUP :], r

        def emit_near(i, value):
            mixed[pl.ds((i - 1) * GROUP, GROUP), lanes] = value

        def emit_far(i, value):
            mixed[pl.ds((inner + i - 1) * GROUP, GROUP), lanes] = value

        stencil(taps_ref, vec_ref.at[0], lanes, near, 1, inner, emit_near)
        stencil(taps_ref, vec_ref.at[0], lanes, far, 1, inner, emit_far)

    each_tile(width, tile)
    gain, nbias = vec_ref.at[1], vec_ref.at[2]
    normalize(mixed, half, gain, nbias, near_ref)
    normalize(mixed.at[pl.ds(half, half)], half, gain, nbias, far_ref)


def edges_kernel(x_ref, sides_ref, up_ref, down_ref, taps_ref, vec_ref, out_ref, mixed):
    rows, cols, width = x_ref.shape
    place = lax.broadcasted_iota(jnp.int32, (cols, LANES), 0)

    def tile(lanes):
        lefts, rights = halves(sides_ref, rows, lanes)
        up, down = up_ref[:, lanes].astype(F32), down_ref[:, lanes].astype(F32)

        def cells(i):
            if i < 0:
                x, l, r = up[:cols], up[cols : cols + 1], up[cols + 1 :]
            elif i == rows:
                x, l, r = down[:cols], down[cols : cols + 1], down[cols + 1 :]
            else:
                x, l, r = x_ref[i, :, lanes].astype(F32), lefts[i : i + 1], rights[i : i + 1]
            return (
                jnp.where(place == 0, l, pltpu.roll(x, 1, 0)),
                x,
                jnp.where(place == cols - 1, r, pltpu.roll(x, cols - 1, 0)),
            )

        def emit(i, value):
            for g in range(cols // GROUP):
                at = 2 * g * GROUP + (GROUP if i else 0)
                mixed[pl.ds(at, GROUP), lanes] = value[g * GROUP : (g + 1) * GROUP]

        stencil(taps_ref, vec_ref.at[0], lanes, cells, 0, 1, emit)
        stencil(taps_ref, vec_ref.at[0], lanes, cells, rows - 1, 1, emit)

    each_tile(width, tile)
    normalize(mixed, 2 * cols, vec_ref.at[1], vec_ref.at[2], out_ref)


def project_kernel(rows, plan, count, fresh, step, side_count, *refs):
    parts, (w_ref, b_ref), refs = refs[:count], refs[count : count + 2], refs[count + 2 :]
    if not fresh:
        refs = refs[1:]
    out_ref, sums, blocks, sems = refs
    heads = w_ref.shape[1] // HD
    width = w_ref.shape[2]
    total = 3 * heads * HD
    block = GROUP * HD
    weight = w_ref[...].reshape(total, width)
    bias = jnp.concatenate([b_ref[pl.ds(t, 1), :].astype(F32) for t in range(3)], axis=1)
    owner = lax.rem(lax.axis_index("cols") + 2 * step, side_count)
    copies = []
    for g, (pieces, other, group) in enumerate(plan):
        rows_of = [parts[ref][pl.ds(at, size), :] for ref, at, size in pieces]
        acc = (
            lax.dot_general(
                jnp.concatenate(rows_of, axis=0),
                weight,
                (((1,), (1,)), ((), ())),
                preferred_element_type=F32,
            )
            + bias
        )
        inner = acc.shape[0] - 2 * GROUP
        for k in range(0, total, LANES):
            piece = acc[:, k : k + LANES]
            span = pl.ds(0, piece.shape[1])
            sums[g % 2, k // LANES, pl.ds(GROUP, inner), span] = piece[:inner]
            sums[g % 2, k // LANES, pl.ds(0, GROUP), span] = piece[inner : inner + GROUP]
            sums[g % 2, k // LANES, pl.ds(inner + GROUP, GROUP), span] = piece[inner + GROUP :]
        position = owner ^ 1 if other else owner
        lane = pl.multiple_of(position * (out_ref.shape[3] // side_count) + group * block, LANES)
        for t in range(3):
            for h in range(heads):
                start = (t * heads + h) * HD
                lo, hi = start // LANES, (start + HD - 1) // LANES + 1
                cells = []
                for j in range(GROUP):
                    tiles = [sums[g % 2, k, pl.ds(j, rows, stride=GROUP), :] for k in range(lo, hi)]
                    cell = tiles[0] if len(tiles) == 1 else jnp.concatenate(tiles, axis=1)
                    cells.append(cell[:, start - lo * LANES : start - lo * LANES + HD])
                blocks[g, t, h] = jnp.concatenate(cells, axis=1).astype(BF16)
            copy = pltpu.make_async_copy(
                blocks.at[g, t], out_ref.at[t, :, :, pl.ds(lane, block)], sems.at[g, t]
            )
            copy.start()
            copies.append(copy)
    for copy in copies:
        copy.wait()


def project(out, parts, plan, step, weight, bias, rows, side_count, shape):
    count = len(parts)
    heads = weight.shape[1] // HD
    fresh = out is None
    operands = [*parts, weight, bias] + ([] if fresh else [out])
    return call(
        functools.partial(project_kernel, rows, plan, count, fresh, step, side_count),
        "project",
        jax.ShapeDtypeStruct(shape, BF16),
        [VMEM] * (count + 2) + ([] if fresh else [HBM]),
        HBM,
        [
            pltpu.VMEM((2, pl.cdiv(3 * heads * HD, LANES), rows * GROUP, LANES), F32),
            pltpu.VMEM((len(plan), 3, heads, rows, GROUP * HD), BF16),
            pltpu.SemaphoreType.DMA((len(plan), 3)),
        ],
        aliases={} if fresh else {len(operands) - 1: 0},
    )(*operands)


def local(patches, conv_taps, conv_bias, norm_gain, norm_bias, qkv_weight, qkv_bias):
    rows, cols, width = patches.shape
    up_count, side_count = lax.axis_size("rows"), lax.axis_size("cols")
    chips = side_count // 2
    wide = cols - 2 * GROUP
    inner = rows - 2
    half = inner * GROUP
    early = EARLY
    few = early * wide
    two = 2 * GROUP
    steps = range(1, chips)

    def array(*shape, dtype=BF16):
        return jax.ShapeDtypeStruct(shape, dtype)

    def across(value):
        return [
            lax.ppermute(value, "cols", [(q, (q + 2 * step) % side_count) for q in range(side_count)])
            for step in steps
        ]

    def swap(value):
        return lax.ppermute(value, "cols", [(q, q ^ 1) for q in range(side_count)])

    def shift(value, axis, count, step):
        return lax.ppermute(value, axis, [(i, i + step) for i in range(count) if 0 <= i + step < count])

    def after(values, others):
        joined = lax.optimization_barrier((*values, *others))
        return list(joined[: len(values)])

    def in_hbm(value):
        return pltpu.with_memory_space_constraint(value, pltpu.HBM)

    first, beside, x, taps, vectors = call(
        functools.partial(first_kernel, early),
        "first",
        [
            array(few + rows, width),
            array(rows, width),
            array(rows, cols, width),
            array(3, 3, width, dtype=F32),
            array(3, 1, width, dtype=F32),
        ],
        [HBM] * 5,
        [VMEM] * 5,
        [pltpu.VMEM((few, width), F32)] + [pltpu.VMEM((width,), F32)] * 3 + [pltpu.SemaphoreType.DMA((6,))],
    )(*[in_hbm(v) for v in (patches, conv_taps, conv_bias, norm_gain, norm_bias)])
    got_first = across(first)

    second = call(
        functools.partial(second_kernel, early + 1),
        "second",
        array(half - few, width),
        [VMEM] * 3,
        VMEM,
        [pltpu.VMEM((half - few, width), F32)],
    )(x, taps, vectors)
    got_second = across(second)

    sides = swap(
        call(
            relay_kernel,
            "relay",
            array(2 * rows, width),
            [VMEM] * 4,
            VMEM,
            [],
        )(beside, got_first[0], got_first[-1], second)
    )

    near, far, top, bottom = call(
        sides_kernel,
        "sides",
        [array(half, width)] * 2 + [array(cols + 2, width)] * 2,
        [VMEM] * 4,
        [VMEM] * 4,
        [pltpu.VMEM((rows, width), F32)] * 2 + [pltpu.VMEM((2 * half, width), F32)],
    )(x, sides, taps, vectors)
    up = shift(bottom, "rows", up_count, 1)
    down = shift(top, "rows", up_count, -1)
    got_near = across(near)
    up, down = after((up, down), got_second)
    edge = call(
        edges_kernel,
        "edges",
        array(2 * cols, width),
        [VMEM] * 6,
        VMEM,
        [pltpu.VMEM((2 * cols, width), F32)],
    )(x, sides, up, down, taps, vectors)
    got_edge = across(edge)
    got_far = across(far)

    shape = (3, qkv_weight.shape[2] // HD, rows, side_count * cols * HD)
    weight = jnp.swapaxes(qkv_weight, 1, 2)
    run = functools.partial(project, weight=weight, bias=qkv_bias, rows=rows, side_count=side_count, shape=shape)

    def cut(value):
        return [value[at : at + PIECE] for at in range(0, value.shape[0], PIECE)]

    def plan(groups, other):
        arrays, entries = [], []
        for group, pieces in groups:
            entry = []
            for value, at, size in pieces:
                entry.append((len(arrays), at, size))
                arrays.append(value)
            entries.append((tuple(entry), other, group))
        return arrays, entries

    def whole(values):
        return [(value, 0, value.shape[0]) for value in values]

    def groups_of(near, first, second, edge, far):
        return [
            (0, whole(near) + [(edge, 0, two)]),
            (1, [(first, 0, few)] + whole(second) + [(edge, two, two)]),
            (2, whole(far) + [(edge, 2 * two, two)]),
        ]

    def step_on(out, groups, other, step):
        arrays, entries = plan(groups, other)
        return run(out, arrays, entries, step)

    out = step_on(None, groups_of([near], first, [second], edge, [far]), 0, 0)
    other_edge = edge
    theirs = groups_of([swap(near)], swap(first), [swap(second)], swap(other_edge), [swap(far)])
    out = step_on(out, theirs, 1, 0)
    for step in steps:
        mine = [v[step - 1] for v in (got_near, got_first, got_second, got_edge)]
        *mine, out = lax.optimization_barrier((*mine, out))
        near, first, second, edge = mine
        other = [swap(v) for v in cut(near)], swap(first), [swap(v) for v in cut(second)], swap(edge)
        out = step_on(out, groups_of([near], first, [second], edge, [])[:2], 0, chips - step)
        out = step_on(out, groups_of(*other, [])[:2], 1, chips - step)
        far, out = lax.optimization_barrier((got_far[step - 1], out))
        out = step_on(out, groups_of([], first, [], edge, [far])[2:], 0, chips - step)
        out = step_on(out, groups_of([], first, [], other[3], [swap(far)])[2:], 1, chips - step)
    return out


def solution(mesh):
    placed = (P("rows", "cols", None), P(), P(), P(), P(), P(None, None, "cols"), P(None, "cols"))
    return jax.shard_map(
        local, mesh=mesh, in_specs=placed, out_specs=P(None, "cols", "rows", None), check_vma=False
    )
```

```python
import functools

import jax
import jax.numpy as jnp
from jax import lax
from jax.experimental import pallas as pl
from jax.experimental.pallas import tpu as pltpu
from jax.sharding import PartitionSpec as P

HD = 80
GROUP = 8
LANES = 128
EPS = 1e-06
VMEM_LIMIT = 32 * 1024 * 1024
K = {'early': 8, 'piece': 96, 'pieceA': 64, 'bsplit': 0, 'csplit': 0, 'A2': 'edges', 'B': 'X', 'C1': None, 'D': None, 'swA': 'X', 'swB': 'X', 'swD': 'X', 'z': 2, 'y': 2}
BF16 = jnp.bfloat16
F32 = jnp.float32

VMEM = pl.BlockSpec(memory_space=pltpu.VMEM)
HBM = pl.BlockSpec(memory_space=pltpu.HBM)


def call(body, name, outs, specs, out_specs, scratch, aliases=None):
    return pl.pallas_call(
        body,
        out_shape=outs,
        in_specs=specs,
        out_specs=out_specs,
        scratch_shapes=scratch,
        input_output_aliases=aliases or {},
        compiler_params=pltpu.CompilerParams(vmem_limit_bytes=VMEM_LIMIT),
        cost_estimate=pl.CostEstimate(flops=1024, bytes_accessed=1024, transcendentals=0),
        name=name,
    )


def stencil(taps_ref, bias_ref, lanes, cells, first, count, emit):
    taps = [[taps_ref[a, pl.ds(b, 1), lanes] for b in range(3)] for a in range(3)]
    bias = bias_ref[:, lanes]
    above = here = None
    for i in range(first - 1, first + count + 1):
        l, c, r = cells(i)
        part = [taps[a][0] * l + taps[a][1] * c + taps[a][2] * r for a in range(3)]
        if i > first:
            emit(i - 1, above + part[2])
        if i >= first:
            above = here + (part[1] + c)
        here = part[0] + bias


def normalize(mixed, count, gain_ref, nbias_ref, out_ref):
    width = mixed.shape[1]
    tiles = [pl.ds(k, LANES) for k in range(0, width, LANES)]
    total = mixed[:count, tiles[0]]
    for lanes in tiles[1:]:
        total = total + mixed[:count, lanes]
    mean = jnp.sum(total, axis=1, keepdims=True) * (1.0 / width)
    square = None
    for lanes in tiles:
        centered = mixed[:count, lanes] - mean
        square = centered * centered if square is None else square + centered * centered
    scale = lax.rsqrt(jnp.sum(square, axis=1, keepdims=True) * (1.0 / width) + EPS)
    for lanes in tiles:
        value = (mixed[:count, lanes] - mean) * scale * gain_ref[:, lanes] + nbias_ref[:, lanes]
        out_ref[:count, lanes] = value.astype(BF16)


def each_tile(width, body):
    def step(k, _):
        body(pl.ds(pl.multiple_of(k * LANES, LANES), LANES))
        return 0

    lax.fori_loop(0, width // LANES, step, 0)


def middle_cells(x_ref, lanes, span):
    cols = x_ref.shape[1]

    def cells(i):
        x = x_ref[i, :, lanes].astype(F32)
        return pltpu.roll(x, 1, 0)[span], x[span], pltpu.roll(x, cols - 1, 0)[span]

    return cells


def core_of(cols_axis):
    return lax.rem(lax.axis_index(cols_axis), 2)


def first_kernel(count, x_hbm, taps_hbm, cbias_hbm, gain_hbm, nbias_hbm, out_ref, inner_ref, x_ref, taps_ref, vec_ref, mixed, *rest):
    *flat, sems = rest
    rows, cols, width = x_ref.shape
    need = count + 2
    copies = [
        pltpu.make_async_copy(x_hbm.at[pl.ds(0, need)], x_ref.at[pl.ds(0, need)], sems.at[0]),
        pltpu.make_async_copy(taps_hbm, taps_ref, sems.at[1]),
        pltpu.make_async_copy(cbias_hbm, flat[0], sems.at[2]),
        pltpu.make_async_copy(gain_hbm, flat[1], sems.at[3]),
        pltpu.make_async_copy(nbias_hbm, flat[2], sems.at[4]),
        pltpu.make_async_copy(x_hbm.at[pl.ds(need, rows - need)], x_ref.at[pl.ds(need, rows - need)], sems.at[5]),
    ]
    for copy in copies:
        copy.start()
    for copy in copies[:-1]:
        copy.wait()
    for k in range(3):
        vec_ref[k] = flat[k][...].reshape(1, width)
    span = slice(GROUP, cols - GROUP)
    wide = cols - 2 * GROUP

    def tile(lanes):
        def emit(i, value):
            mixed[pl.ds((i - 1) * wide, wide), lanes] = value

        stencil(taps_ref, vec_ref.at[0], lanes, middle_cells(x_ref, lanes, span), 1, count, emit)

    each_tile(width, tile)
    normalize(mixed, count * wide, vec_ref.at[1], vec_ref.at[2], out_ref)
    copies[-1].wait()
    core = core_of("cols")

    def sides(lanes):
        left = [x_ref[i, pl.ds(0, GROUP), lanes].astype(F32)[:1] for i in range(rows)]
        right = [x_ref[i, pl.ds(cols - GROUP, GROUP), lanes].astype(F32)[GROUP - 1 :] for i in range(rows)]
        left, right = jnp.concatenate(left, axis=0), jnp.concatenate(right, axis=0)
        out_ref[count * wide :, lanes] = jnp.where(core == 1, right, left).astype(BF16)
        inner_ref[:, lanes] = jnp.where(core == 1, left, right).astype(BF16)

    each_tile(width, sides)


def second_kernel(start, x_ref, taps_ref, vec_ref, out_ref, mixed):
    rows, cols, width = x_ref.shape
    span = slice(GROUP, cols - GROUP)
    wide = cols - 2 * GROUP
    count = rows - 1 - start

    def tile(lanes):
        def emit(i, value):
            mixed[pl.ds((i - start) * wide, wide), lanes] = value

        stencil(taps_ref, vec_ref.at[0], lanes, middle_cells(x_ref, lanes, span), start, count, emit)

    each_tile(width, tile)
    normalize(mixed, count * wide, vec_ref.at[1], vec_ref.at[2], out_ref)


def relay_kernel(beside_ref, before_ref, behind_ref, _, out_ref):
    rows = beside_ref.shape[0]
    few = before_ref.shape[0] - rows
    col, count = lax.axis_index("cols"), lax.axis_size("cols")
    core = core_of("cols")
    none = jnp.logical_or(col == 1, col == count - 2)
    out_ref[:rows, :] = beside_ref[...]
    passed = jnp.where(core == 1, before_ref[few:, :].astype(F32), behind_ref[few:, :].astype(F32))
    out_ref[rows:, :] = jnp.where(none, 0.0, passed).astype(BF16)


def halves(sides_ref, rows, lanes):
    other, passed = sides_ref[:rows, lanes].astype(F32), sides_ref[rows:, lanes].astype(F32)
    core = core_of("cols")
    return jnp.where(core == 1, other, passed), jnp.where(core == 1, passed, other)


def ends_kernel(x_ref, sides_ref, pair_ref, cross_ref):
    rows, cols, _ = x_ref.shape
    lefts, rights = halves(sides_ref, rows, slice(None))
    odd = lax.rem(lax.axis_index("rows"), 2) == 1

    for ref, at in ((pair_ref, (0, rows - 1)), (cross_ref, (rows - 1, 0))):
        ref[:cols, :] = jnp.where(odd, x_ref[at[0]].astype(F32), x_ref[at[1]].astype(F32)).astype(BF16)
        ends = [
            jnp.where(odd, column[at[0] : at[0] + 1], column[at[1] : at[1] + 1]) for column in (lefts, rights)
        ]
        ref[cols:, :] = jnp.concatenate(ends, axis=0).astype(BF16)


def sides_kernel(
    x_ref, sides_ref, taps_ref, vec_ref, *refs
):
    rows, cols, width = x_ref.shape
    place = lax.broadcasted_iota(jnp.int32, (GROUP, LANES), 0)
    *outs, lefts, rights, mixed = refs
    inner = rows - 2
    half = inner * GROUP
    lefts[...], rights[...] = halves(sides_ref, rows, slice(None))
    def tile(lanes):
        def near(i):
            x = x_ref[i, :, lanes].astype(F32)
            here, both = x[:GROUP], x[: 2 * GROUP]
            l = jnp.where(place == 0, lefts[pl.ds(i, 1), lanes], pltpu.roll(here, 1, 0))
            return l, here, pltpu.roll(both, 2 * GROUP - 1, 0)[:GROUP]

        def far(i):
            x = x_ref[i, :, lanes].astype(F32)
            here, both = x[cols - GROUP :], x[cols - 2 * GROUP :]
            r = jnp.where(place == GROUP - 1, rights[pl.ds(i, 1), lanes], pltpu.roll(here, GROUP - 1, 0))
            return pltpu.roll(both, 1, 0)[GROUP:], here, r

        def emit_near(i, value):
            mixed[pl.ds((i - 1) * GROUP, GROUP), lanes] = value

        def emit_far(i, value):
            mixed[pl.ds((inner + i - 1) * GROUP, GROUP), lanes] = value

        stencil(taps_ref, vec_ref.at[0], lanes, near, 1, inner, emit_near)
        stencil(taps_ref, vec_ref.at[0], lanes, far, 1, inner, emit_far)

    each_tile(width, tile)
    gain, nbias = vec_ref.at[1], vec_ref.at[2]
    base = 0
    for ref in outs:
        count = ref.shape[0]
        normalize(mixed.at[pl.ds(base, count)], count, gain, nbias, ref)
        base += count


def edges_kernel(x_ref, sides_ref, pair_ref, cross_ref, taps_ref, vec_ref, out_ref, mixed):
    rows, cols, width = x_ref.shape
    place = lax.broadcasted_iota(jnp.int32, (cols, LANES), 0)
    odd = lax.rem(lax.axis_index("rows"), 2) == 1

    def tile(lanes):
        lefts, rights = halves(sides_ref, rows, lanes)
        pair, cross = pair_ref[:, lanes].astype(F32), cross_ref[:, lanes].astype(F32)
        up, down = jnp.where(odd, pair, cross), jnp.where(odd, cross, pair)

        def cells(i):
            if i < 0:
                x, l, r = up[:cols], up[cols : cols + 1], up[cols + 1 :]
            elif i == rows:
                x, l, r = down[:cols], down[cols : cols + 1], down[cols + 1 :]
            else:
                x, l, r = x_ref[i, :, lanes].astype(F32), lefts[i : i + 1], rights[i : i + 1]
            return (
                jnp.where(place == 0, l, pltpu.roll(x, 1, 0)),
                x,
                jnp.where(place == cols - 1, r, pltpu.roll(x, cols - 1, 0)),
            )

        def emit(i, value):
            for g in range(cols // GROUP):
                at = 2 * g * GROUP + (GROUP if i else 0)
                mixed[pl.ds(at, GROUP), lanes] = value[g * GROUP : (g + 1) * GROUP]

        stencil(taps_ref, vec_ref.at[0], lanes, cells, 0, 1, emit)
        stencil(taps_ref, vec_ref.at[0], lanes, cells, rows - 1, 1, emit)

    each_tile(width, tile)
    normalize(mixed, 2 * cols, vec_ref.at[1], vec_ref.at[2], out_ref)


def project_kernel(rows, plan, count, fresh, step, side_count, *refs):
    parts, (w_ref, b_ref), refs = refs[:count], refs[count : count + 2], refs[count + 2 :]
    if not fresh:
        refs = refs[1:]
    out_ref, sums, blocks, sems = refs
    heads = w_ref.shape[1] // HD
    width = w_ref.shape[2]
    total = 3 * heads * HD
    block = GROUP * HD
    weight = w_ref[...].reshape(total, width)
    bias = jnp.concatenate([b_ref[pl.ds(t, 1), :].astype(F32) for t in range(3)], axis=1)
    owner = lax.rem(lax.axis_index("cols") + 2 * step, side_count)
    side = rows * GROUP
    for batch in batches_of(len(plan)):
        pieces = [parts[ref][pl.ds(at, size), :] for g in batch for ref, at, size in plan[g][0]]
        acc = (
            lax.dot_general(
                jnp.concatenate(pieces, axis=0), weight, (((1,), (1,)), ((), ())), preferred_element_type=F32
            )
            + bias
        )
        inner = side - 2 * GROUP
        for n, g in enumerate(batch):
            for k in range(0, total, LANES):
                piece = acc[n * side : (n + 1) * side, k : k + LANES]
                span = pl.ds(0, piece.shape[1])
                sums[g, k // LANES, pl.ds(GROUP, inner), span] = piece[:inner]
                sums[g, k // LANES, pl.ds(0, GROUP), span] = piece[inner : inner + GROUP]
                sums[g, k // LANES, pl.ds(inner + GROUP, GROUP), span] = piece[inner + GROUP :]
    copies = []
    for g, (_, other, group) in enumerate(plan):
        position = owner ^ 1 if other else owner
        lane = pl.multiple_of(position * (out_ref.shape[3] // side_count) + group * block, LANES)
        for t in range(3):
            for h in range(heads):
                start = (t * heads + h) * HD
                lo, hi = start // LANES, (start + HD - 1) // LANES + 1
                cells = []
                for j in range(GROUP):
                    tiles = [sums[g, k, pl.ds(j, rows, stride=GROUP), :] for k in range(lo, hi)]
                    cell = tiles[0] if len(tiles) == 1 else jnp.concatenate(tiles, axis=1)
                    cells.append(cell[:, start - lo * LANES : start - lo * LANES + HD])
                blocks[g, t, h] = jnp.concatenate(cells, axis=1).astype(BF16)
            copy = pltpu.make_async_copy(
                blocks.at[g, t], out_ref.at[t, :, :, pl.ds(lane, block)], sems.at[g, t]
            )
            copy.start()
            copies.append(copy)
    for copy in copies:
        copy.wait()


def batches_of(count):
    size = 3 if count % 3 == 0 else 2
    return [range(at, min(at + size, count)) for at in range(0, count, size)]


def project(out, parts, plan, step, weight, bias, rows, side_count, shape):
    count = len(parts)
    heads = weight.shape[1] // HD
    fresh = out is None
    operands = [*parts, weight, bias] + ([] if fresh else [out])
    return call(
        functools.partial(project_kernel, rows, plan, count, fresh, step, side_count),
        "project",
        jax.ShapeDtypeStruct(shape, BF16),
        [VMEM] * (count + 2) + ([] if fresh else [HBM]),
        HBM,
        [
            pltpu.VMEM((len(plan), pl.cdiv(3 * heads * HD, LANES), rows * GROUP, LANES), F32),
            pltpu.VMEM((len(plan), 3, heads, rows, GROUP * HD), BF16),
            pltpu.SemaphoreType.DMA((len(plan), 3)),
        ],
        aliases={} if fresh else {len(operands) - 1: 0},
    )(*operands)


def local(patches, conv_taps, conv_bias, norm_gain, norm_bias, qkv_weight, qkv_bias):
    rows, cols, width = patches.shape
    up_count, side_count = lax.axis_size("rows"), lax.axis_size("cols")
    chips = side_count // 2
    wide = cols - 2 * GROUP
    inner = rows - 2
    half = inner * GROUP
    early = K['early']
    few = early * wide
    two = 2 * GROUP
    steps = range(1, chips)

    def array(*shape, dtype=BF16):
        return jax.ShapeDtypeStruct(shape, dtype)

    def across(value):
        return [
            lax.ppermute(value, "cols", [(q, (q + 2 * step) % side_count) for q in range(side_count)])
            for step in steps
        ]

    def swap(value):
        return lax.ppermute(value, "cols", [(q, q ^ 1) for q in range(side_count)])

    def exchange(value, start):
        pairs = [(i, i + 1) for i in range(start, up_count - 1, 2)]
        return lax.ppermute(value, "rows", pairs + [(j, i) for i, j in pairs])

    def after(values, others):
        joined = lax.optimization_barrier((*values, *others))
        return list(joined[: len(values)])

    def in_hbm(value):
        return pltpu.with_memory_space_constraint(value, pltpu.HBM)

    first, beside, x, taps, vectors = call(
        functools.partial(first_kernel, early),
        "first",
        [
            array(few + rows, width),
            array(rows, width),
            array(rows, cols, width),
            array(3, 3, width, dtype=F32),
            array(3, 1, width, dtype=F32),
        ],
        [HBM] * 5,
        [VMEM] * 5,
        [pltpu.VMEM((few, width), F32)] + [pltpu.VMEM((width,), F32)] * 3 + [pltpu.SemaphoreType.DMA((6,))],
    )(*[in_hbm(v) for v in (patches, conv_taps, conv_bias, norm_gain, norm_bias)])
    got_first = across(first)

    second = call(
        functools.partial(second_kernel, early + 1),
        "second",
        array(half - few, width),
        [VMEM] * 3,
        VMEM,
        [pltpu.VMEM((half - few, width), F32)],
    )(x, taps, vectors)
    got_second = across(second)

    sides = swap(
        call(
            relay_kernel,
            "relay",
            array(2 * rows, width),
            [VMEM] * 4,
            VMEM,
            [],
        )(beside, got_first[0], got_first[-1], second)
    )

    def cuts(size):
        return [size, half - size] if size else [half]

    sizes = cuts(K["bsplit"]) + cuts(K["csplit"])
    pair, cross = call(
        ends_kernel,
        "ends",
        [array(cols + 2, width)] * 2,
        [VMEM] * 2,
        [VMEM] * 2,
        [],
    )(x, sides)
    parts = call(
        sides_kernel,
        "sides",
        [array(size, width) for size in sizes],
        [VMEM] * 4,
        [VMEM] * len(sizes),
        [pltpu.VMEM((rows, width), F32)] * 2 + [pltpu.VMEM((2 * half, width), F32)],
    )(x, sides, taps, vectors)
    count = len(cuts(K["bsplit"]))
    near, far = parts[:count], parts[count:]
    got_near = [across(v) for v in near]
    got_far = [across(v) for v in far]
    marks = {"A2": got_second, "B": sum(got_near, []), "C1": got_far[0]}

    def hold(place, values):
        others = sum([marks[k] for k in marks if K[k] == place], [])
        return after(values, others) if others else list(values)

    pair, cross = hold("up", (pair, cross))
    pair, cross = exchange(pair, 0), exchange(cross, 1)
    pair, cross = hold("edges", (pair, cross))
    edge = call(
        edges_kernel,
        "edges",
        array(2 * cols, width),
        [VMEM] * 6,
        VMEM,
        [pltpu.VMEM((2 * cols, width), F32)],
    )(x, sides, pair, cross, taps, vectors)
    got_edge = across(edge)
    marks["D"] = got_edge

    shape = (3, qkv_weight.shape[2] // HD, rows, side_count * cols * HD)
    weight = jnp.swapaxes(qkv_weight, 1, 2)
    run = functools.partial(project, weight=weight, bias=qkv_bias, rows=rows, side_count=side_count, shape=shape)

    def whole(values):
        return [(value, 0, value.shape[0]) for value in values]

    def groups_of(near, first, second, edge, far, other):
        return [
            (whole(near) + [(edge, 0, two)], other, 0),
            ([(first, 0, few)] + whole(second) + [(edge, two, two)], other, 1),
            (whole(far) + [(edge, 2 * two, two)], other, 2),
        ]

    def step_on(out, groups, step):
        arrays, entries = [], []
        for pieces, other, group in groups:
            entry = []
            for value, at, size in pieces:
                entry.append((len(arrays), at, size))
                arrays.append(value)
            entries.append((tuple(entry), other, group))
        return run(out, arrays, entries, step)

    (late,) = hold("eswap", (edge,))
    (held,) = hold("X", (first,))
    out = step_on(
        None,
        groups_of(near, held, [second], edge, far, 0)
        + groups_of([swap(v) for v in near], swap(first), [swap(second)], swap(late), [swap(v) for v in far], 1),
        0,
    )
    for step in steps:
        at = step - 1
        pick = dict(
            swA=[got_first[at], got_second[at]], swB=[v[at] for v in got_near], swD=[got_edge[at]]
        )
        for key in pick:
            if K[key] == "X":
                *pick[key], out = lax.optimization_barrier((*pick[key], out))
        c1 = [v[at] for v in got_far]
        if K["C1"] == "dswap":
            pick["swD"] = after(pick["swD"], c1[:1])
        (got1, got2), gotb, (gote,) = pick["swA"], pick["swB"], pick["swD"]
        other_near = [swap(v[p : p + K["piece"]]) for v in gotb for p in range(0, v.shape[0], K["piece"])]
        other1, other2, othere = swap(got1), swap(got2), swap(gote)
        mine = groups_of(gotb, got1, [got2], gote, [], 0)[:2]
        theirs = groups_of(other_near, other1, [other2], othere, [], 1)[:2]
        if K["y"] == 2:
            out = step_on(out, mine, chips - step)
            out = step_on(out, theirs, chips - step)
        else:
            out = step_on(out, mine + theirs, chips - step)
        *c1, out = lax.optimization_barrier((*c1, out))
        last = groups_of([], got1, [], gote, c1, 0)[2:]
        other = groups_of([], got1, [], othere, [swap(v) for v in c1], 1)[2:]
        if K["z"] == 2:
            out = step_on(out, last, chips - step)
            out = step_on(out, other, chips - step)
        else:
            out = step_on(out, last + other, chips - step)
    return out


def solution(mesh):
    placed = (P("rows", "cols", None), P(), P(), P(), P(), P(None, None, "cols"), P(None, "cols"))
    return jax.shard_map(
        local, mesh=mesh, in_specs=placed, out_specs=P(None, "cols", "rows", None), check_vma=False
    )
```

```python
import functools

import jax
import jax.numpy as jnp
from jax import lax
from jax.experimental import pallas as pl
from jax.experimental.pallas import tpu as pltpu
from jax.sharding import PartitionSpec as P

HD = 80
GROUP = 8
LANES = 128
EPS = 1e-06
VMEM_LIMIT = 32 * 1024 * 1024
K = {'piece': 96, 'pieceA': 96, 'bsplit': 0, 'csplit': 0, 'A2': 'edges', 'B': None, 'C1': None, 'D': None, 'swA': 'X', 'swB': 'X', 'swD': 'X', 'z': 2, 'y': 2}
BF16 = jnp.bfloat16
F32 = jnp.float32

VMEM = pl.BlockSpec(memory_space=pltpu.VMEM)
HBM = pl.BlockSpec(memory_space=pltpu.HBM)


def call(body, name, outs, specs, out_specs, scratch, aliases=None):
    return pl.pallas_call(
        body,
        out_shape=outs,
        in_specs=specs,
        out_specs=out_specs,
        scratch_shapes=scratch,
        input_output_aliases=aliases or {},
        compiler_params=pltpu.CompilerParams(vmem_limit_bytes=VMEM_LIMIT),
        cost_estimate=pl.CostEstimate(flops=1024, bytes_accessed=1024, transcendentals=0),
        name=name,
    )


def stencil(taps_ref, bias_ref, lanes, cells, first, count, emit):
    taps = [[taps_ref[a, pl.ds(b, 1), lanes] for b in range(3)] for a in range(3)]
    bias = bias_ref[:, lanes]
    above = here = None
    for i in range(first - 1, first + count + 1):
        l, c, r = cells(i)
        part = [taps[a][0] * l + taps[a][1] * c + taps[a][2] * r for a in range(3)]
        if i > first:
            emit(i - 1, above + part[2])
        if i >= first:
            above = here + (part[1] + c)
        here = part[0] + bias


def normalize(mixed, count, gain_ref, nbias_ref, out_ref):
    width = mixed.shape[1]
    tiles = [pl.ds(k, LANES) for k in range(0, width, LANES)]
    total = mixed[:count, tiles[0]]
    for lanes in tiles[1:]:
        total = total + mixed[:count, lanes]
    mean = jnp.sum(total, axis=1, keepdims=True) * (1.0 / width)
    square = None
    for lanes in tiles:
        centered = mixed[:count, lanes] - mean
        square = centered * centered if square is None else square + centered * centered
    scale = lax.rsqrt(jnp.sum(square, axis=1, keepdims=True) * (1.0 / width) + EPS)
    for lanes in tiles:
        value = (mixed[:count, lanes] - mean) * scale * gain_ref[:, lanes] + nbias_ref[:, lanes]
        out_ref[:count, lanes] = value.astype(BF16)


def each_tile(width, body):
    def step(k, _):
        body(pl.ds(pl.multiple_of(k * LANES, LANES), LANES))
        return 0

    lax.fori_loop(0, width // LANES, step, 0)


def middle_cells(x_ref, lanes, span):
    cols = x_ref.shape[1]

    def cells(i):
        x = x_ref[i, :, lanes].astype(F32)
        return pltpu.roll(x, 1, 0)[span], x[span], pltpu.roll(x, cols - 1, 0)[span]

    return cells


def core_of(cols_axis):
    return lax.rem(lax.axis_index(cols_axis), 2)


def first_kernel(x_hbm, taps_hbm, cbias_hbm, gain_hbm, nbias_hbm, outer_ref, inner_ref, x_ref, taps_ref, vec_ref, *rest):
    *flat, sems = rest
    rows, cols, width = x_ref.shape
    pairs = ((x_hbm, x_ref), (taps_hbm, taps_ref), (cbias_hbm, flat[0]), (gain_hbm, flat[1]), (nbias_hbm, flat[2]))
    copies = [pltpu.make_async_copy(source, target, sems.at[k]) for k, (source, target) in enumerate(pairs)]
    for copy in copies:
        copy.start()
    for copy in copies:
        copy.wait()
    for k, ref in enumerate(flat):
        vec_ref[k] = ref[...].reshape(1, width)
    core = core_of("cols")

    def sides(lanes):
        left = [x_ref[i, pl.ds(0, GROUP), lanes].astype(F32)[:1] for i in range(rows)]
        right = [x_ref[i, pl.ds(cols - GROUP, GROUP), lanes].astype(F32)[GROUP - 1 :] for i in range(rows)]
        left, right = jnp.concatenate(left, axis=0), jnp.concatenate(right, axis=0)
        outer_ref[:, lanes] = jnp.where(core == 1, right, left).astype(BF16)
        inner_ref[:, lanes] = jnp.where(core == 1, left, right).astype(BF16)

    each_tile(width, sides)


def middle_kernel(x_ref, taps_ref, vec_ref, out_ref, mixed):
    rows, cols, width = x_ref.shape
    start = 1
    span = slice(GROUP, cols - GROUP)
    wide = cols - 2 * GROUP
    count = rows - 1 - start

    def tile(lanes):
        def emit(i, value):
            mixed[pl.ds((i - start) * wide, wide), lanes] = value

        stencil(taps_ref, vec_ref.at[0], lanes, middle_cells(x_ref, lanes, span), start, count, emit)

    each_tile(width, tile)
    normalize(mixed, count * wide, vec_ref.at[1], vec_ref.at[2], out_ref)


def relay_kernel(beside_ref, before_ref, behind_ref, _, out_ref):
    rows = beside_ref.shape[0]
    col, count = lax.axis_index("cols"), lax.axis_size("cols")
    core = core_of("cols")
    none = jnp.logical_or(col == 1, col == count - 2)
    out_ref[:rows, :] = beside_ref[...]
    passed = jnp.where(core == 1, before_ref[...].astype(F32), behind_ref[...].astype(F32))
    out_ref[rows:, :] = jnp.where(none, 0.0, passed).astype(BF16)


def halves(sides_ref, rows, lanes):
    other, passed = sides_ref[:rows, lanes].astype(F32), sides_ref[rows:, lanes].astype(F32)
    core = core_of("cols")
    return jnp.where(core == 1, other, passed), jnp.where(core == 1, passed, other)


def ends_kernel(x_ref, sides_ref, pair_ref, cross_ref):
    rows, cols, _ = x_ref.shape
    lefts, rights = halves(sides_ref, rows, slice(None))
    odd = lax.rem(lax.axis_index("rows"), 2) == 1

    for ref, at in ((pair_ref, (0, rows - 1)), (cross_ref, (rows - 1, 0))):
        ref[:cols, :] = jnp.where(odd, x_ref[at[0]].astype(F32), x_ref[at[1]].astype(F32)).astype(BF16)
        ends = [
            jnp.where(odd, column[at[0] : at[0] + 1], column[at[1] : at[1] + 1]) for column in (lefts, rights)
        ]
        ref[cols:, :] = jnp.concatenate(ends, axis=0).astype(BF16)


def sides_kernel(
    x_ref, sides_ref, taps_ref, vec_ref, *refs
):
    rows, cols, width = x_ref.shape
    place = lax.broadcasted_iota(jnp.int32, (GROUP, LANES), 0)
    *outs, lefts, rights, mixed = refs
    inner = rows - 2
    half = inner * GROUP
    lefts[...], rights[...] = halves(sides_ref, rows, slice(None))
    def tile(lanes):
        def near(i):
            x = x_ref[i, :, lanes].astype(F32)
            here, both = x[:GROUP], x[: 2 * GROUP]
            l = jnp.where(place == 0, lefts[pl.ds(i, 1), lanes], pltpu.roll(here, 1, 0))
            return l, here, pltpu.roll(both, 2 * GROUP - 1, 0)[:GROUP]

        def far(i):
            x = x_ref[i, :, lanes].astype(F32)
            here, both = x[cols - GROUP :], x[cols - 2 * GROUP :]
            r = jnp.where(place == GROUP - 1, rights[pl.ds(i, 1), lanes], pltpu.roll(here, GROUP - 1, 0))
            return pltpu.roll(both, 1, 0)[GROUP:], here, r

        def emit_near(i, value):
            mixed[pl.ds((i - 1) * GROUP, GROUP), lanes] = value

        def emit_far(i, value):
            mixed[pl.ds((inner + i - 1) * GROUP, GROUP), lanes] = value

        stencil(taps_ref, vec_ref.at[0], lanes, near, 1, inner, emit_near)
        stencil(taps_ref, vec_ref.at[0], lanes, far, 1, inner, emit_far)

    each_tile(width, tile)
    gain, nbias = vec_ref.at[1], vec_ref.at[2]
    base = 0
    for ref in outs:
        count = ref.shape[0]
        normalize(mixed.at[pl.ds(base, count)], count, gain, nbias, ref)
        base += count


def edges_kernel(x_ref, sides_ref, pair_ref, cross_ref, taps_ref, vec_ref, out_ref, mixed):
    rows, cols, width = x_ref.shape
    place = lax.broadcasted_iota(jnp.int32, (cols, LANES), 0)
    odd = lax.rem(lax.axis_index("rows"), 2) == 1

    def tile(lanes):
        lefts, rights = halves(sides_ref, rows, lanes)
        pair, cross = pair_ref[:, lanes].astype(F32), cross_ref[:, lanes].astype(F32)
        up, down = jnp.where(odd, pair, cross), jnp.where(odd, cross, pair)

        def cells(i):
            if i < 0:
                x, l, r = up[:cols], up[cols : cols + 1], up[cols + 1 :]
            elif i == rows:
                x, l, r = down[:cols], down[cols : cols + 1], down[cols + 1 :]
            else:
                x, l, r = x_ref[i, :, lanes].astype(F32), lefts[i : i + 1], rights[i : i + 1]
            return (
                jnp.where(place == 0, l, pltpu.roll(x, 1, 0)),
                x,
                jnp.where(place == cols - 1, r, pltpu.roll(x, cols - 1, 0)),
            )

        def emit(i, value):
            for g in range(cols // GROUP):
                at = 2 * g * GROUP + (GROUP if i else 0)
                mixed[pl.ds(at, GROUP), lanes] = value[g * GROUP : (g + 1) * GROUP]

        stencil(taps_ref, vec_ref.at[0], lanes, cells, 0, 1, emit)
        stencil(taps_ref, vec_ref.at[0], lanes, cells, rows - 1, 1, emit)

    each_tile(width, tile)
    normalize(mixed, 2 * cols, vec_ref.at[1], vec_ref.at[2], out_ref)


def project_kernel(rows, plan, count, fresh, step, side_count, *refs):
    parts, (w_ref, b_ref), refs = refs[:count], refs[count : count + 2], refs[count + 2 :]
    if not fresh:
        refs = refs[1:]
    out_ref, sums, blocks, sems = refs
    heads = w_ref.shape[1] // HD
    width = w_ref.shape[2]
    total = 3 * heads * HD
    block = GROUP * HD
    weight = w_ref[...].reshape(total, width)
    bias = jnp.concatenate([b_ref[pl.ds(t, 1), :].astype(F32) for t in range(3)], axis=1)
    owner = lax.rem(lax.axis_index("cols") + 2 * step, side_count)
    side = rows * GROUP
    for batch in batches_of(len(plan)):
        pieces = [parts[ref][pl.ds(at, size), :] for g in batch for ref, at, size in plan[g][0]]
        acc = (
            lax.dot_general(
                jnp.concatenate(pieces, axis=0), weight, (((1,), (1,)), ((), ())), preferred_element_type=F32
            )
            + bias
        )
        inner = side - 2 * GROUP
        for n, g in enumerate(batch):
            for k in range(0, total, LANES):
                piece = acc[n * side : (n + 1) * side, k : k + LANES]
                span = pl.ds(0, piece.shape[1])
                sums[g, k // LANES, pl.ds(GROUP, inner), span] = piece[:inner]
                sums[g, k // LANES, pl.ds(0, GROUP), span] = piece[inner : inner + GROUP]
                sums[g, k // LANES, pl.ds(inner + GROUP, GROUP), span] = piece[inner + GROUP :]
    copies = []
    for g, (_, other, group) in enumerate(plan):
        position = owner ^ 1 if other else owner
        lane = pl.multiple_of(position * (out_ref.shape[3] // side_count) + group * block, LANES)
        for t in range(3):
            for h in range(heads):
                start = (t * heads + h) * HD
                lo, hi = start // LANES, (start + HD - 1) // LANES + 1
                cells = []
                for j in range(GROUP):
                    tiles = [sums[g, k, pl.ds(j, rows, stride=GROUP), :] for k in range(lo, hi)]
                    cell = tiles[0] if len(tiles) == 1 else jnp.concatenate(tiles, axis=1)
                    cells.append(cell[:, start - lo * LANES : start - lo * LANES + HD])
                blocks[g, t, h] = jnp.concatenate(cells, axis=1).astype(BF16)
            copy = pltpu.make_async_copy(
                blocks.at[g, t], out_ref.at[t, :, :, pl.ds(lane, block)], sems.at[g, t]
            )
            copy.start()
            copies.append(copy)
    for copy in copies:
        copy.wait()


def batches_of(count):
    size = 3 if count % 3 == 0 else 2
    return [range(at, min(at + size, count)) for at in range(0, count, size)]


def project(out, parts, plan, step, weight, bias, rows, side_count, shape):
    count = len(parts)
    heads = weight.shape[1] // HD
    fresh = out is None
    operands = [*parts, weight, bias] + ([] if fresh else [out])
    return call(
        functools.partial(project_kernel, rows, plan, count, fresh, step, side_count),
        "project",
        jax.ShapeDtypeStruct(shape, BF16),
        [VMEM] * (count + 2) + ([] if fresh else [HBM]),
        HBM,
        [
            pltpu.VMEM((len(plan), pl.cdiv(3 * heads * HD, LANES), rows * GROUP, LANES), F32),
            pltpu.VMEM((len(plan), 3, heads, rows, GROUP * HD), BF16),
            pltpu.SemaphoreType.DMA((len(plan), 3)),
        ],
        aliases={} if fresh else {len(operands) - 1: 0},
    )(*operands)


def local(patches, conv_taps, conv_bias, norm_gain, norm_bias, qkv_weight, qkv_bias):
    rows, cols, width = patches.shape
    up_count, side_count = lax.axis_size("rows"), lax.axis_size("cols")
    chips = side_count // 2
    wide = cols - 2 * GROUP
    inner = rows - 2
    half = inner * GROUP
    two = 2 * GROUP
    steps = range(1, chips)

    def array(*shape, dtype=BF16):
        return jax.ShapeDtypeStruct(shape, dtype)

    def across(value):
        return [
            lax.ppermute(value, "cols", [(q, (q + 2 * step) % side_count) for q in range(side_count)])
            for step in steps
        ]

    def swap(value):
        return lax.ppermute(value, "cols", [(q, q ^ 1) for q in range(side_count)])

    def exchange(value, start):
        pairs = [(i, i + 1) for i in range(start, up_count - 1, 2)]
        return lax.ppermute(value, "rows", pairs + [(j, i) for i, j in pairs])

    def after(values, others):
        joined = lax.optimization_barrier((*values, *others))
        return list(joined[: len(values)])

    def in_hbm(value):
        return pltpu.with_memory_space_constraint(value, pltpu.HBM)

    outer, beside, x, taps, vectors = call(
        first_kernel,
        "first",
        [
            array(rows, width),
            array(rows, width),
            array(rows, cols, width),
            array(3, 3, width, dtype=F32),
            array(3, 1, width, dtype=F32),
        ],
        [HBM] * 5,
        [VMEM] * 5,
        [pltpu.VMEM((width,), F32)] * 3 + [pltpu.SemaphoreType.DMA((5,))],
    )(*[in_hbm(v) for v in (patches, conv_taps, conv_bias, norm_gain, norm_bias)])
    got_outer = across(outer)

    middle = call(
        middle_kernel,
        "middle",
        array(half, width),
        [VMEM] * 3,
        VMEM,
        [pltpu.VMEM((half, width), F32)],
    )(x, taps, vectors)
    got_middle = across(middle)

    sides = swap(
        call(
            relay_kernel,
            "relay",
            array(2 * rows, width),
            [VMEM] * 4,
            VMEM,
            [],
        )(beside, got_outer[0], got_outer[-1], middle)
    )

    def cuts(size):
        return [size, half - size] if size else [half]

    sizes = cuts(K["bsplit"]) + cuts(K["csplit"])
    pair, cross = call(
        ends_kernel,
        "ends",
        [array(cols + 2, width)] * 2,
        [VMEM] * 2,
        [VMEM] * 2,
        [],
    )(x, sides)
    parts = call(
        sides_kernel,
        "sides",
        [array(size, width) for size in sizes],
        [VMEM] * 4,
        [VMEM] * len(sizes),
        [pltpu.VMEM((rows, width), F32)] * 2 + [pltpu.VMEM((2 * half, width), F32)],
    )(x, sides, taps, vectors)
    count = len(cuts(K["bsplit"]))
    near, far = parts[:count], parts[count:]
    got_near = [across(v) for v in near]
    got_far = [across(v) for v in far]
    marks = {"A2": got_middle, "B": sum(got_near, []), "C1": got_far[0]}

    def hold(place, values):
        others = sum([marks[k] for k in marks if K[k] == place], [])
        return after(values, others) if others else list(values)

    pair, cross = hold("up", (pair, cross))
    pair, cross = exchange(pair, 0), exchange(cross, 1)
    pair, cross = hold("edges", (pair, cross))
    edge = call(
        edges_kernel,
        "edges",
        array(2 * cols, width),
        [VMEM] * 6,
        VMEM,
        [pltpu.VMEM((2 * cols, width), F32)],
    )(x, sides, pair, cross, taps, vectors)
    got_edge = across(edge)
    marks["D"] = got_edge

    shape = (3, qkv_weight.shape[2] // HD, rows, side_count * cols * HD)
    weight = jnp.swapaxes(qkv_weight, 1, 2)
    run = functools.partial(project, weight=weight, bias=qkv_bias, rows=rows, side_count=side_count, shape=shape)

    def whole(values):
        return [(value, 0, value.shape[0]) for value in values]

    def groups_of(near, middle, edge, far, other):
        return [
            (whole(near) + [(edge, 0, two)], other, 0),
            (whole(middle) + [(edge, two, two)], other, 1),
            (whole(far) + [(edge, 2 * two, two)], other, 2),
        ]

    def step_on(out, groups, step):
        arrays, entries = [], []
        for pieces, other, group in groups:
            entry = []
            for value, at, size in pieces:
                entry.append((len(arrays), at, size))
                arrays.append(value)
            entries.append((tuple(entry), other, group))
        return run(out, arrays, entries, step)

    (late,) = hold("eswap", (edge,))
    (held,) = hold("X", (middle,))
    out = step_on(
        None,
        groups_of(near, [held], edge, far, 0)
        + groups_of([swap(v) for v in near], [swap(middle)], swap(late), [swap(v) for v in far], 1),
        0,
    )
    for step in steps:
        at = step - 1
        pick = dict(
            swA=[got_middle[at]], swB=[v[at] for v in got_near], swD=[got_edge[at]]
        )
        for key in pick:
            if K[key] == "X":
                *pick[key], out = lax.optimization_barrier((*pick[key], out))
        c1 = [v[at] for v in got_far]
        if K["C1"] == "dswap":
            pick["swD"] = after(pick["swD"], c1[:1])
        gota, gotb, (gote,) = pick["swA"], pick["swB"], pick["swD"]
        other_near = [swap(v[p : p + K["piece"]]) for v in gotb for p in range(0, v.shape[0], K["piece"])]
        other_middle = [swap(v[p : p + K["pieceA"]]) for v in gota for p in range(0, v.shape[0], K["pieceA"])]
        othere = swap(gote)
        mine = groups_of(gotb, gota, gote, [], 0)[:2]
        theirs = groups_of(other_near, other_middle, othere, [], 1)[:2]
        if K["y"] == 2:
            out = step_on(out, mine, chips - step)
            out = step_on(out, theirs, chips - step)
        else:
            out = step_on(out, mine + theirs, chips - step)
        *c1, out = lax.optimization_barrier((*c1, out))
        last = groups_of([], [], gote, c1, 0)[2:]
        other = groups_of([], [], othere, [swap(v) for v in c1], 1)[2:]
        if K["z"] == 2:
            out = step_on(out, last, chips - step)
            out = step_on(out, other, chips - step)
        else:
            out = step_on(out, last + other, chips - step)
    return out


def solution(mesh):
    placed = (P("rows", "cols", None), P(), P(), P(), P(), P(None, None, "cols"), P(None, "cols"))
    return jax.shard_map(
        local, mesh=mesh, in_specs=placed, out_specs=P(None, "cols", "rows", None), check_vma=False
    )
```

```python
import functools

import jax
import jax.numpy as jnp
from jax import lax
from jax.experimental import pallas as pl
from jax.experimental.pallas import tpu as pltpu
from jax.sharding import PartitionSpec as P

HD = 80
GROUP = 8
LANES = 128
EPS = 1e-06
VMEM_LIMIT = 32 * 1024 * 1024
K = {'extra': 32, 'early': 8, 'piece': 96, 'pieceA': 96, 'bsplit': 0, 'csplit': 0, 'A2': 'edges', 'B': None, 'C1': None, 'D': None, 'swA': 'X', 'swB': 'X', 'swD': 'X', 'z': 2, 'y': 2}
BF16 = jnp.bfloat16
F32 = jnp.float32

VMEM = pl.BlockSpec(memory_space=pltpu.VMEM)
HBM = pl.BlockSpec(memory_space=pltpu.HBM)


def call(body, name, outs, specs, out_specs, scratch, aliases=None):
    return pl.pallas_call(
        body,
        out_shape=outs,
        in_specs=specs,
        out_specs=out_specs,
        scratch_shapes=scratch,
        input_output_aliases=aliases or {},
        compiler_params=pltpu.CompilerParams(vmem_limit_bytes=VMEM_LIMIT),
        cost_estimate=pl.CostEstimate(flops=1024, bytes_accessed=1024, transcendentals=0),
        name=name,
    )


def stencil(taps_ref, bias_ref, lanes, cells, first, count, emit):
    taps = [[taps_ref[a, pl.ds(b, 1), lanes] for b in range(3)] for a in range(3)]
    bias = bias_ref[:, lanes]
    above = here = None
    for i in range(first - 1, first + count + 1):
        l, c, r = cells(i)
        part = [taps[a][0] * l + taps[a][1] * c + taps[a][2] * r for a in range(3)]
        if i > first:
            emit(i - 1, above + part[2])
        if i >= first:
            above = here + (part[1] + c)
        here = part[0] + bias


def normalize(mixed, count, gain_ref, nbias_ref, out_ref):
    width = mixed.shape[1]
    tiles = [pl.ds(k, LANES) for k in range(0, width, LANES)]
    total = mixed[:count, tiles[0]]
    for lanes in tiles[1:]:
        total = total + mixed[:count, lanes]
    mean = jnp.sum(total, axis=1, keepdims=True) * (1.0 / width)
    square = None
    for lanes in tiles:
        centered = mixed[:count, lanes] - mean
        square = centered * centered if square is None else square + centered * centered
    scale = lax.rsqrt(jnp.sum(square, axis=1, keepdims=True) * (1.0 / width) + EPS)
    for lanes in tiles:
        value = (mixed[:count, lanes] - mean) * scale * gain_ref[:, lanes] + nbias_ref[:, lanes]
        out_ref[:count, lanes] = value.astype(BF16)


def each_tile(width, body):
    def step(k, _):
        body(pl.ds(pl.multiple_of(k * LANES, LANES), LANES))
        return 0

    lax.fori_loop(0, width // LANES, step, 0)


def middle_cells(x_ref, lanes, span):
    cols = x_ref.shape[1]

    def cells(i):
        x = x_ref[i, :, lanes].astype(F32)
        return pltpu.roll(x, 1, 0)[span], x[span], pltpu.roll(x, cols - 1, 0)[span]

    return cells


def core_of(cols_axis):
    return lax.rem(lax.axis_index(cols_axis), 2)


def column(x_ref, first, count, last, lanes):
    cols = x_ref.shape[1]
    part = pl.multiple_of(jnp.where(last, cols - GROUP, 0), GROUP)
    cells = [x_ref[i, pl.ds(part, GROUP), lanes].astype(F32) for i in range(first, first + count)]
    cells = [jnp.where(last, cell[GROUP - 1 :], cell[:1]) for cell in cells]
    return jnp.concatenate(cells, axis=0).astype(BF16)


def first_kernel(x_hbm, taps_hbm, cbias_hbm, gain_hbm, nbias_hbm, outer_ref, x_ref, taps_ref, vec_ref, *rest):
    *flat, sems = rest
    rows, _, width = x_ref.shape
    spans = [pl.ds(at, GROUP) for at in range(0, rows, GROUP)]
    pairs = [(x_hbm.at[span], x_ref.at[span]) for span in spans]
    pairs += [(taps_hbm, taps_ref), (cbias_hbm, flat[0]), (gain_hbm, flat[1]), (nbias_hbm, flat[2])]
    copies = [pltpu.make_async_copy(source, target, sems.at[k]) for k, (source, target) in enumerate(pairs)]
    for copy in copies:
        copy.start()
    last = core_of("cols") == 1
    for k, span in enumerate(spans):
        copies[k].wait()
        for at in range(0, width, LANES):
            lanes = pl.ds(at, LANES)
            outer_ref[span, lanes] = column(x_ref, k * GROUP, GROUP, last, lanes)
    for copy in copies[len(spans) :]:
        copy.wait()
    for k, ref in enumerate(flat):
        vec_ref[k] = ref[...].reshape(1, width)


def middle_kernel(x_ref, taps_ref, vec_ref, out_ref, inner_ref, mixed):
    rows, cols, width = x_ref.shape
    start = 1
    span = slice(GROUP, cols - GROUP)
    wide = cols - 2 * GROUP
    count = rows - 1 - start

    def tile(lanes):
        def emit(i, value):
            mixed[pl.ds((i - start) * wide, wide), lanes] = value

        stencil(taps_ref, vec_ref.at[0], lanes, middle_cells(x_ref, lanes, span), start, count, emit)
        inner_ref[:, lanes] = column(x_ref, 0, rows, core_of("cols") == 0, lanes)

    each_tile(width, tile)
    normalize(mixed, count * wide, vec_ref.at[1], vec_ref.at[2], out_ref)


def relay_kernel(beside_ref, before_ref, behind_ref, out_ref):
    rows = beside_ref.shape[0]
    col, count = lax.axis_index("cols"), lax.axis_size("cols")
    core = core_of("cols")
    none = jnp.logical_or(col == 1, col == count - 2)
    out_ref[:rows, :] = beside_ref[...]
    passed = jnp.where(core == 1, before_ref[...].astype(F32), behind_ref[...].astype(F32))
    out_ref[rows:, :] = jnp.where(none, 0.0, passed).astype(BF16)


def halves(sides_ref, rows, lanes):
    other, passed = sides_ref[:rows, lanes].astype(F32), sides_ref[rows:, lanes].astype(F32)
    core = core_of("cols")
    return jnp.where(core == 1, other, passed), jnp.where(core == 1, passed, other)


def ends_kernel(x_ref, sides_ref, pair_ref, cross_ref):
    rows, cols, _ = x_ref.shape
    lefts, rights = halves(sides_ref, rows, slice(None))
    odd = lax.rem(lax.axis_index("rows"), 2) == 1

    for ref, at in ((pair_ref, (0, rows - 1)), (cross_ref, (rows - 1, 0))):
        ref[:cols, :] = jnp.where(odd, x_ref[at[0]].astype(F32), x_ref[at[1]].astype(F32)).astype(BF16)
        ends = [
            jnp.where(odd, column[at[0] : at[0] + 1], column[at[1] : at[1] + 1]) for column in (lefts, rights)
        ]
        ref[cols:, :] = jnp.concatenate(ends, axis=0).astype(BF16)


def sides_kernel(
    x_ref, sides_ref, taps_ref, vec_ref, *refs
):
    rows, cols, width = x_ref.shape
    place = lax.broadcasted_iota(jnp.int32, (GROUP, LANES), 0)
    *outs, lefts, rights, mixed = refs
    inner = rows - 2
    half = inner * GROUP
    lefts[...], rights[...] = halves(sides_ref, rows, slice(None))
    def tile(lanes):
        def near(i):
            x = x_ref[i, :, lanes].astype(F32)
            here, both = x[:GROUP], x[: 2 * GROUP]
            l = jnp.where(place == 0, lefts[pl.ds(i, 1), lanes], pltpu.roll(here, 1, 0))
            return l, here, pltpu.roll(both, 2 * GROUP - 1, 0)[:GROUP]

        def far(i):
            x = x_ref[i, :, lanes].astype(F32)
            here, both = x[cols - GROUP :], x[cols - 2 * GROUP :]
            r = jnp.where(place == GROUP - 1, rights[pl.ds(i, 1), lanes], pltpu.roll(here, GROUP - 1, 0))
            return pltpu.roll(both, 1, 0)[GROUP:], here, r

        def emit_near(i, value):
            mixed[pl.ds((i - 1) * GROUP, GROUP), lanes] = value

        def emit_far(i, value):
            mixed[pl.ds((inner + i - 1) * GROUP, GROUP), lanes] = value

        stencil(taps_ref, vec_ref.at[0], lanes, near, 1, inner, emit_near)
        stencil(taps_ref, vec_ref.at[0], lanes, far, 1, inner, emit_far)

    each_tile(width, tile)
    gain, nbias = vec_ref.at[1], vec_ref.at[2]
    base = 0
    for ref in outs:
        count = ref.shape[0]
        normalize(mixed.at[pl.ds(base, count)], count, gain, nbias, ref)
        base += count


def edges_kernel(x_ref, sides_ref, pair_ref, cross_ref, taps_ref, vec_ref, out_ref, mixed):
    rows, cols, width = x_ref.shape
    place = lax.broadcasted_iota(jnp.int32, (cols, LANES), 0)
    odd = lax.rem(lax.axis_index("rows"), 2) == 1

    def tile(lanes):
        lefts, rights = halves(sides_ref, rows, lanes)
        pair, cross = pair_ref[:, lanes].astype(F32), cross_ref[:, lanes].astype(F32)
        up, down = jnp.where(odd, pair, cross), jnp.where(odd, cross, pair)

        def cells(i):
            if i < 0:
                x, l, r = up[:cols], up[cols : cols + 1], up[cols + 1 :]
            elif i == rows:
                x, l, r = down[:cols], down[cols : cols + 1], down[cols + 1 :]
            else:
                x, l, r = x_ref[i, :, lanes].astype(F32), lefts[i : i + 1], rights[i : i + 1]
            return (
                jnp.where(place == 0, l, pltpu.roll(x, 1, 0)),
                x,
                jnp.where(place == cols - 1, r, pltpu.roll(x, cols - 1, 0)),
            )

        def emit(i, value):
            for g in range(cols // GROUP):
                at = 2 * g * GROUP + (GROUP if i else 0)
                mixed[pl.ds(at, GROUP), lanes] = value[g * GROUP : (g + 1) * GROUP]

        stencil(taps_ref, vec_ref.at[0], lanes, cells, 0, 1, emit)
        stencil(taps_ref, vec_ref.at[0], lanes, cells, rows - 1, 1, emit)

    each_tile(width, tile)
    normalize(mixed, 2 * cols, vec_ref.at[1], vec_ref.at[2], out_ref)


def project_kernel(rows, plan, count, fresh, step, side_count, *refs):
    parts, (w_ref, b_ref), refs = refs[:count], refs[count : count + 2], refs[count + 2 :]
    if not fresh:
        refs = refs[1:]
    out_ref, sums, blocks, sems = refs
    heads = w_ref.shape[1] // HD
    width = w_ref.shape[2]
    total = 3 * heads * HD
    block = GROUP * HD
    weight = w_ref[...].reshape(total, width)
    bias = jnp.concatenate([b_ref[pl.ds(t, 1), :].astype(F32) for t in range(3)], axis=1)
    owner = lax.rem(lax.axis_index("cols") + 2 * step, side_count)
    side = rows * GROUP
    for batch in batches_of(len(plan)):
        pieces = [parts[ref][pl.ds(at, size), :] for g in batch for ref, at, size in plan[g][0]]
        acc = (
            lax.dot_general(
                jnp.concatenate(pieces, axis=0), weight, (((1,), (1,)), ((), ())), preferred_element_type=F32
            )
            + bias
        )
        inner = side - 2 * GROUP
        for n, g in enumerate(batch):
            for k in range(0, total, LANES):
                piece = acc[n * side : (n + 1) * side, k : k + LANES]
                span = pl.ds(0, piece.shape[1])
                sums[g, k // LANES, pl.ds(GROUP, inner), span] = piece[:inner]
                sums[g, k // LANES, pl.ds(0, GROUP), span] = piece[inner : inner + GROUP]
                sums[g, k // LANES, pl.ds(inner + GROUP, GROUP), span] = piece[inner + GROUP :]
    copies = []
    for g, (_, other, group) in enumerate(plan):
        position = owner ^ 1 if other else owner
        lane = pl.multiple_of(position * (out_ref.shape[3] // side_count) + group * block, LANES)
        for t in range(3):
            for h in range(heads):
                start = (t * heads + h) * HD
                lo, hi = start // LANES, (start + HD - 1) // LANES + 1
                cells = []
                for j in range(GROUP):
                    tiles = [sums[g, k, pl.ds(j, rows, stride=GROUP), :] for k in range(lo, hi)]
                    cell = tiles[0] if len(tiles) == 1 else jnp.concatenate(tiles, axis=1)
                    cells.append(cell[:, start - lo * LANES : start - lo * LANES + HD])
                blocks[g, t, h] = jnp.concatenate(cells, axis=1).astype(BF16)
            copy = pltpu.make_async_copy(
                blocks.at[g, t], out_ref.at[t, :, :, pl.ds(lane, block)], sems.at[g, t]
            )
            copy.start()
            copies.append(copy)
    for copy in copies:
        copy.wait()


def batches_of(count):
    size = 3 if count % 3 == 0 else 2
    return [range(at, min(at + size, count)) for at in range(0, count, size)]


def project(out, parts, plan, step, weight, bias, rows, side_count, shape):
    count = len(parts)
    heads = weight.shape[1] // HD
    fresh = out is None
    operands = [*parts, weight, bias] + ([] if fresh else [out])
    return call(
        functools.partial(project_kernel, rows, plan, count, fresh, step, side_count),
        "project",
        jax.ShapeDtypeStruct(shape, BF16),
        [VMEM] * (count + 2) + ([] if fresh else [HBM]),
        HBM,
        [
            pltpu.VMEM((len(plan), pl.cdiv(3 * heads * HD, LANES), rows * GROUP, LANES), F32),
            pltpu.VMEM((len(plan), 3, heads, rows, GROUP * HD), BF16),
            pltpu.SemaphoreType.DMA((len(plan), 3)),
        ],
        aliases={} if fresh else {len(operands) - 1: 0},
    )(*operands)


def local(patches, conv_taps, conv_bias, norm_gain, norm_bias, qkv_weight, qkv_bias):
    rows, cols, width = patches.shape
    up_count, side_count = lax.axis_size("rows"), lax.axis_size("cols")
    chips = side_count // 2
    wide = cols - 2 * GROUP
    inner = rows - 2
    half = inner * GROUP
    two = 2 * GROUP
    steps = range(1, chips)

    def array(*shape, dtype=BF16):
        return jax.ShapeDtypeStruct(shape, dtype)

    def across(value):
        return [
            lax.ppermute(value, "cols", [(q, (q + 2 * step) % side_count) for q in range(side_count)])
            for step in steps
        ]

    def swap(value):
        return lax.ppermute(value, "cols", [(q, q ^ 1) for q in range(side_count)])

    def exchange(value, start):
        pairs = [(i, i + 1) for i in range(start, up_count - 1, 2)]
        return lax.ppermute(value, "rows", pairs + [(j, i) for i, j in pairs])

    def after(values, others):
        joined = lax.optimization_barrier((*values, *others))
        return list(joined[: len(values)])

    def in_hbm(value):
        return pltpu.with_memory_space_constraint(value, pltpu.HBM)

    outer, x, taps, vectors = call(
        first_kernel,
        "first",
        [
            array(rows, width),
            array(rows, cols, width),
            array(3, 3, width, dtype=F32),
            array(3, 1, width, dtype=F32),
        ],
        [HBM] * 5,
        [VMEM] * 4,
        [pltpu.VMEM((width,), F32)] * 3 + [pltpu.SemaphoreType.DMA((rows // GROUP + 4,))],
    )(*[in_hbm(v) for v in (patches, conv_taps, conv_bias, norm_gain, norm_bias)])
    got_outer = across(outer)

    middle, beside = call(
        middle_kernel,
        "middle",
        [array(half, width), array(rows, width)],
        [VMEM] * 3,
        [VMEM] * 2,
        [pltpu.VMEM((half, width), F32)],
    )(x, taps, vectors)
    got_middle = across(middle)

    sides = swap(
        call(
            relay_kernel,
            "relay",
            array(2 * rows, width),
            [VMEM] * 3,
            VMEM,
            [],
        )(beside, got_outer[0], got_outer[-1])
    )

    def cuts(size):
        return [size, half - size] if size else [half]

    sizes = cuts(K["bsplit"]) + cuts(K["csplit"])
    pair, cross = call(
        ends_kernel,
        "ends",
        [array(cols + 2, width)] * 2,
        [VMEM] * 2,
        [VMEM] * 2,
        [],
    )(x, sides)
    parts = call(
        sides_kernel,
        "sides",
        [array(size, width) for size in sizes],
        [VMEM] * 4,
        [VMEM] * len(sizes),
        [pltpu.VMEM((rows, width), F32)] * 2 + [pltpu.VMEM((2 * half, width), F32)],
    )(x, sides, taps, vectors)
    count = len(cuts(K["bsplit"]))
    near, far = parts[:count], parts[count:]
    got_near = [across(v) for v in near]
    got_far = [across(v) for v in far]
    marks = {"A2": got_middle, "B": sum(got_near, []), "C1": got_far[0]}

    def hold(place, values):
        others = sum([marks[k] for k in marks if K[k] == place], [])
        return after(values, others) if others else list(values)

    pair, cross = hold("up", (pair, cross))
    pair, cross = exchange(pair, 0), exchange(cross, 1)
    pair, cross = hold("edges", (pair, cross))
    edge = call(
        edges_kernel,
        "edges",
        array(2 * cols, width),
        [VMEM] * 6,
        VMEM,
        [pltpu.VMEM((2 * cols, width), F32)],
    )(x, sides, pair, cross, taps, vectors)
    got_edge = across(edge)
    marks["D"] = got_edge

    shape = (3, qkv_weight.shape[2] // HD, rows, side_count * cols * HD)
    weight = jnp.swapaxes(qkv_weight, 1, 2)
    run = functools.partial(project, weight=weight, bias=qkv_bias, rows=rows, side_count=side_count, shape=shape)

    def whole(values):
        return [(value, 0, value.shape[0]) for value in values]

    def groups_of(near, middle, edge, far, other):
        return [
            (whole(near) + [(edge, 0, two)], other, 0),
            (whole(middle) + [(edge, two, two)], other, 1),
            (whole(far) + [(edge, 2 * two, two)], other, 2),
        ]

    def step_on(out, groups, step):
        arrays, entries = [], []
        for pieces, other, group in groups:
            entry = []
            for value, at, size in pieces:
                entry.append((len(arrays), at, size))
                arrays.append(value)
            entries.append((tuple(entry), other, group))
        return run(out, arrays, entries, step)

    (late,) = hold("eswap", (edge,))
    (held,) = hold("X", (middle,))
    out = step_on(
        None,
        groups_of(near, [held], edge, far, 0)
        + groups_of([swap(v) for v in near], [swap(middle)], swap(late), [swap(v) for v in far], 1),
        0,
    )
    for step in steps:
        at = step - 1
        pick = dict(
            swA=[got_middle[at]], swB=[v[at] for v in got_near], swD=[got_edge[at]]
        )
        for key in pick:
            if K[key] == "X":
                *pick[key], out = lax.optimization_barrier((*pick[key], out))
        c1 = [v[at] for v in got_far]
        if K["C1"] == "dswap":
            pick["swD"] = after(pick["swD"], c1[:1])
        gota, gotb, (gote,) = pick["swA"], pick["swB"], pick["swD"]
        other_near = [swap(v[p : p + K["piece"]]) for v in gotb for p in range(0, v.shape[0], K["piece"])]
        other_middle = [swap(v[p : p + K["pieceA"]]) for v in gota for p in range(0, v.shape[0], K["pieceA"])]
        othere = swap(gote)
        mine = groups_of(gotb, gota, gote, [], 0)[:2]
        theirs = groups_of(other_near, other_middle, othere, [], 1)[:2]
        if K["y"] == 2:
            out = step_on(out, mine, chips - step)
            out = step_on(out, theirs, chips - step)
        else:
            out = step_on(out, mine + theirs, chips - step)
        *c1, out = lax.optimization_barrier((*c1, out))
        last = groups_of([], [], gote, c1, 0)[2:]
        other = groups_of([], [], othere, [swap(v) for v in c1], 1)[2:]
        if K["z"] == 2:
            out = step_on(out, last, chips - step)
            out = step_on(out, other, chips - step)
        else:
            out = step_on(out, last + other, chips - step)
    return out


def solution(mesh):
    placed = (P("rows", "cols", None), P(), P(), P(), P(), P(None, None, "cols"), P(None, "cols"))
    return jax.shard_map(
        local, mesh=mesh, in_specs=placed, out_specs=P(None, "cols", "rows", None), check_vma=False
    )
```

```python
import functools

import jax
import jax.numpy as jnp
from jax import lax
from jax.experimental import pallas as pl
from jax.experimental.pallas import tpu as pltpu
from jax.sharding import PartitionSpec as P

HD = 80
GROUP = 8
LANES = 128
EPS = 1e-06
VMEM_LIMIT = 32 * 1024 * 1024
K = {'pieceF': 128, 'extra': 32, 'early': 8, 'piece': 96, 'pieceA': 96, 'bsplit': 0, 'csplit': 0, 'A2': 'edges', 'B': None, 'C1': None, 'D': None, 'swA': 'X', 'swB': 'X', 'swD': 'X', 'z': 2, 'y': 2}
BF16 = jnp.bfloat16
F32 = jnp.float32

VMEM = pl.BlockSpec(memory_space=pltpu.VMEM)
HBM = pl.BlockSpec(memory_space=pltpu.HBM)


def call(body, name, outs, specs, out_specs, scratch, aliases=None):
    return pl.pallas_call(
        body,
        out_shape=outs,
        in_specs=specs,
        out_specs=out_specs,
        scratch_shapes=scratch,
        input_output_aliases=aliases or {},
        compiler_params=pltpu.CompilerParams(vmem_limit_bytes=VMEM_LIMIT),
        cost_estimate=pl.CostEstimate(flops=1024, bytes_accessed=1024, transcendentals=0),
        name=name,
    )


def stencil(taps_ref, bias_ref, lanes, cells, first, count, emit):
    taps = [[taps_ref[a, pl.ds(b, 1), lanes] for b in range(3)] for a in range(3)]
    bias = bias_ref[:, lanes]
    above = here = None
    for i in range(first - 1, first + count + 1):
        l, c, r = cells(i)
        part = [taps[a][0] * l + taps[a][1] * c + taps[a][2] * r for a in range(3)]
        if i > first:
            emit(i - 1, above + part[2])
        if i >= first:
            above = here + (part[1] + c)
        here = part[0] + bias


def normalize(mixed, count, gain_ref, nbias_ref, out_ref):
    width = mixed.shape[1]
    tiles = [pl.ds(k, LANES) for k in range(0, width, LANES)]
    total = mixed[:count, tiles[0]]
    for lanes in tiles[1:]:
        total = total + mixed[:count, lanes]
    mean = jnp.sum(total, axis=1, keepdims=True) * (1.0 / width)
    square = None
    for lanes in tiles:
        centered = mixed[:count, lanes] - mean
        square = centered * centered if square is None else square + centered * centered
    scale = lax.rsqrt(jnp.sum(square, axis=1, keepdims=True) * (1.0 / width) + EPS)
    for lanes in tiles:
        value = (mixed[:count, lanes] - mean) * scale * gain_ref[:, lanes] + nbias_ref[:, lanes]
        out_ref[:count, lanes] = value.astype(BF16)


def each_tile(width, body):
    def step(k, _):
        body(pl.ds(pl.multiple_of(k * LANES, LANES), LANES))
        return 0

    lax.fori_loop(0, width // LANES, step, 0)


def middle_cells(x_ref, lanes, span):
    cols = x_ref.shape[1]

    def cells(i):
        x = x_ref[i, :, lanes].astype(F32)
        return pltpu.roll(x, 1, 0)[span], x[span], pltpu.roll(x, cols - 1, 0)[span]

    return cells


def core_of(cols_axis):
    return lax.rem(lax.axis_index(cols_axis), 2)


def column(x_ref, first, count, last, lanes):
    cols = x_ref.shape[1]
    part = pl.multiple_of(jnp.where(last, cols - GROUP, 0), GROUP)
    cells = [x_ref[i, pl.ds(part, GROUP), lanes].astype(F32) for i in range(first, first + count)]
    cells = [jnp.where(last, cell[GROUP - 1 :], cell[:1]) for cell in cells]
    return jnp.concatenate(cells, axis=0).astype(BF16)


def first_kernel(x_hbm, taps_hbm, cbias_hbm, gain_hbm, nbias_hbm, outer_ref, x_ref, taps_ref, vec_ref, *rest):
    *flat, sems = rest
    rows, _, width = x_ref.shape
    spans = [pl.ds(at, GROUP) for at in range(0, rows, GROUP)]
    pairs = [(x_hbm.at[span], x_ref.at[span]) for span in spans]
    pairs += [(taps_hbm, taps_ref), (cbias_hbm, flat[0]), (gain_hbm, flat[1]), (nbias_hbm, flat[2])]
    copies = [pltpu.make_async_copy(source, target, sems.at[k]) for k, (source, target) in enumerate(pairs)]
    for copy in copies:
        copy.start()
    last = core_of("cols") == 1
    for k, span in enumerate(spans):
        copies[k].wait()
        for at in range(0, width, LANES):
            lanes = pl.ds(at, LANES)
            outer_ref[span, lanes] = column(x_ref, k * GROUP, GROUP, last, lanes)
    for copy in copies[len(spans) :]:
        copy.wait()
    for k, ref in enumerate(flat):
        vec_ref[k] = ref[...].reshape(1, width)


def middle_kernel(x_ref, taps_ref, vec_ref, out_ref, inner_ref, mixed):
    rows, cols, width = x_ref.shape
    start = 1
    span = slice(GROUP, cols - GROUP)
    wide = cols - 2 * GROUP
    count = rows - 1 - start

    def tile(lanes):
        def emit(i, value):
            mixed[pl.ds((i - start) * wide, wide), lanes] = value

        stencil(taps_ref, vec_ref.at[0], lanes, middle_cells(x_ref, lanes, span), start, count, emit)
        inner_ref[:, lanes] = column(x_ref, 0, rows, core_of("cols") == 0, lanes)

    each_tile(width, tile)
    normalize(mixed, count * wide, vec_ref.at[1], vec_ref.at[2], out_ref)


def relay_kernel(beside_ref, before_ref, behind_ref, out_ref):
    rows = beside_ref.shape[0]
    col, count = lax.axis_index("cols"), lax.axis_size("cols")
    core = core_of("cols")
    none = jnp.logical_or(col == 1, col == count - 2)
    out_ref[:rows, :] = beside_ref[...]
    passed = jnp.where(core == 1, before_ref[...].astype(F32), behind_ref[...].astype(F32))
    out_ref[rows:, :] = jnp.where(none, 0.0, passed).astype(BF16)


def halves(sides_ref, rows, lanes):
    other, passed = sides_ref[:rows, lanes].astype(F32), sides_ref[rows:, lanes].astype(F32)
    core = core_of("cols")
    return jnp.where(core == 1, other, passed), jnp.where(core == 1, passed, other)


def ends_kernel(x_ref, sides_ref, pair_ref, cross_ref):
    rows, cols, _ = x_ref.shape
    lefts, rights = halves(sides_ref, rows, slice(None))
    odd = lax.rem(lax.axis_index("rows"), 2) == 1

    for ref, at in ((pair_ref, (0, rows - 1)), (cross_ref, (rows - 1, 0))):
        ref[:cols, :] = jnp.where(odd, x_ref[at[0]].astype(F32), x_ref[at[1]].astype(F32)).astype(BF16)
        ends = [
            jnp.where(odd, column[at[0] : at[0] + 1], column[at[1] : at[1] + 1]) for column in (lefts, rights)
        ]
        ref[cols:, :] = jnp.concatenate(ends, axis=0).astype(BF16)


def side_kernel(last, x_ref, sides_ref, taps_ref, vec_ref, out_ref, beside, mixed):
    rows, cols, width = x_ref.shape
    place = lax.broadcasted_iota(jnp.int32, (GROUP, LANES), 0)
    beside[...] = halves(sides_ref, rows, slice(None))[last]

    def tile(lanes):
        def cells(i):
            x = x_ref[i, :, lanes].astype(F32)
            edge = beside[pl.ds(i, 1), lanes]
            if last:
                here, both = x[cols - GROUP :], x[cols - 2 * GROUP :]
                r = jnp.where(place == GROUP - 1, edge, pltpu.roll(here, GROUP - 1, 0))
                return pltpu.roll(both, 1, 0)[GROUP:], here, r
            here, both = x[:GROUP], x[: 2 * GROUP]
            l = jnp.where(place == 0, edge, pltpu.roll(here, 1, 0))
            return l, here, pltpu.roll(both, 2 * GROUP - 1, 0)[:GROUP]

        def emit(i, value):
            mixed[pl.ds((i - 1) * GROUP, GROUP), lanes] = value

        stencil(taps_ref, vec_ref.at[0], lanes, cells, 1, rows - 2, emit)

    each_tile(width, tile)
    normalize(mixed, mixed.shape[0], vec_ref.at[1], vec_ref.at[2], out_ref)


def edges_kernel(x_ref, sides_ref, pair_ref, cross_ref, taps_ref, vec_ref, out_ref, mixed):
    rows, cols, width = x_ref.shape
    place = lax.broadcasted_iota(jnp.int32, (cols, LANES), 0)
    odd = lax.rem(lax.axis_index("rows"), 2) == 1

    def tile(lanes):
        lefts, rights = halves(sides_ref, rows, lanes)
        pair, cross = pair_ref[:, lanes].astype(F32), cross_ref[:, lanes].astype(F32)
        up, down = jnp.where(odd, pair, cross), jnp.where(odd, cross, pair)

        def cells(i):
            if i < 0:
                x, l, r = up[:cols], up[cols : cols + 1], up[cols + 1 :]
            elif i == rows:
                x, l, r = down[:cols], down[cols : cols + 1], down[cols + 1 :]
            else:
                x, l, r = x_ref[i, :, lanes].astype(F32), lefts[i : i + 1], rights[i : i + 1]
            return (
                jnp.where(place == 0, l, pltpu.roll(x, 1, 0)),
                x,
                jnp.where(place == cols - 1, r, pltpu.roll(x, cols - 1, 0)),
            )

        def emit(i, value):
            for g in range(cols // GROUP):
                at = 2 * g * GROUP + (GROUP if i else 0)
                mixed[pl.ds(at, GROUP), lanes] = value[g * GROUP : (g + 1) * GROUP]

        stencil(taps_ref, vec_ref.at[0], lanes, cells, 0, 1, emit)
        stencil(taps_ref, vec_ref.at[0], lanes, cells, rows - 1, 1, emit)

    each_tile(width, tile)
    normalize(mixed, 2 * cols, vec_ref.at[1], vec_ref.at[2], out_ref)


def project_kernel(rows, plan, count, fresh, step, side_count, *refs):
    parts, (w_ref, b_ref), refs = refs[:count], refs[count : count + 2], refs[count + 2 :]
    if not fresh:
        refs = refs[1:]
    out_ref, sums, blocks, sems = refs
    heads = w_ref.shape[1] // HD
    width = w_ref.shape[2]
    total = 3 * heads * HD
    block = GROUP * HD
    weight = w_ref[...].reshape(total, width)
    bias = jnp.concatenate([b_ref[pl.ds(t, 1), :].astype(F32) for t in range(3)], axis=1)
    owner = lax.rem(lax.axis_index("cols") + 2 * step, side_count)
    side = rows * GROUP
    for batch in batches_of(len(plan)):
        pieces = [parts[ref][pl.ds(at, size), :] for g in batch for ref, at, size in plan[g][0]]
        acc = (
            lax.dot_general(
                jnp.concatenate(pieces, axis=0), weight, (((1,), (1,)), ((), ())), preferred_element_type=F32
            )
            + bias
        )
        inner = side - 2 * GROUP
        for n, g in enumerate(batch):
            for k in range(0, total, LANES):
                piece = acc[n * side : (n + 1) * side, k : k + LANES]
                span = pl.ds(0, piece.shape[1])
                sums[g, k // LANES, pl.ds(GROUP, inner), span] = piece[:inner]
                sums[g, k // LANES, pl.ds(0, GROUP), span] = piece[inner : inner + GROUP]
                sums[g, k // LANES, pl.ds(inner + GROUP, GROUP), span] = piece[inner + GROUP :]
    copies = []
    for g, (_, other, group) in enumerate(plan):
        position = owner ^ 1 if other else owner
        lane = pl.multiple_of(position * (out_ref.shape[3] // side_count) + group * block, LANES)
        for t in range(3):
            for h in range(heads):
                start = (t * heads + h) * HD
                lo, hi = start // LANES, (start + HD - 1) // LANES + 1
                cells = []
                for j in range(GROUP):
                    tiles = [sums[g, k, pl.ds(j, rows, stride=GROUP), :] for k in range(lo, hi)]
                    cell = tiles[0] if len(tiles) == 1 else jnp.concatenate(tiles, axis=1)
                    cells.append(cell[:, start - lo * LANES : start - lo * LANES + HD])
                blocks[g, t, h] = jnp.concatenate(cells, axis=1).astype(BF16)
            copy = pltpu.make_async_copy(
                blocks.at[g, t], out_ref.at[t, :, :, pl.ds(lane, block)], sems.at[g, t]
            )
            copy.start()
            copies.append(copy)
    for copy in copies:
        copy.wait()


def batches_of(count):
    size = 3 if count % 3 == 0 else 2
    return [range(at, min(at + size, count)) for at in range(0, count, size)]


def project(out, parts, plan, step, weight, bias, rows, side_count, shape):
    count = len(parts)
    heads = weight.shape[1] // HD
    fresh = out is None
    operands = [*parts, weight, bias] + ([] if fresh else [out])
    return call(
        functools.partial(project_kernel, rows, plan, count, fresh, step, side_count),
        "project",
        jax.ShapeDtypeStruct(shape, BF16),
        [VMEM] * (count + 2) + ([] if fresh else [HBM]),
        HBM,
        [
            pltpu.VMEM((len(plan), pl.cdiv(3 * heads * HD, LANES), rows * GROUP, LANES), F32),
            pltpu.VMEM((len(plan), 3, heads, rows, GROUP * HD), BF16),
            pltpu.SemaphoreType.DMA((len(plan), 3)),
        ],
        aliases={} if fresh else {len(operands) - 1: 0},
    )(*operands)


def local(patches, conv_taps, conv_bias, norm_gain, norm_bias, qkv_weight, qkv_bias):
    rows, cols, width = patches.shape
    up_count, side_count = lax.axis_size("rows"), lax.axis_size("cols")
    chips = side_count // 2
    wide = cols - 2 * GROUP
    inner = rows - 2
    half = inner * GROUP
    two = 2 * GROUP
    steps = range(1, chips)

    def array(*shape, dtype=BF16):
        return jax.ShapeDtypeStruct(shape, dtype)

    def across(value):
        return [
            lax.ppermute(value, "cols", [(q, (q + 2 * step) % side_count) for q in range(side_count)])
            for step in steps
        ]

    def swap(value):
        return lax.ppermute(value, "cols", [(q, q ^ 1) for q in range(side_count)])

    def exchange(value, start):
        pairs = [(i, i + 1) for i in range(start, up_count - 1, 2)]
        return lax.ppermute(value, "rows", pairs + [(j, i) for i, j in pairs])

    def after(values, others):
        joined = lax.optimization_barrier((*values, *others))
        return list(joined[: len(values)])

    def in_hbm(value):
        return pltpu.with_memory_space_constraint(value, pltpu.HBM)

    outer, x, taps, vectors = call(
        first_kernel,
        "first",
        [
            array(rows, width),
            array(rows, cols, width),
            array(3, 3, width, dtype=F32),
            array(3, 1, width, dtype=F32),
        ],
        [HBM] * 5,
        [VMEM] * 4,
        [pltpu.VMEM((width,), F32)] * 3 + [pltpu.SemaphoreType.DMA((rows // GROUP + 4,))],
    )(*[in_hbm(v) for v in (patches, conv_taps, conv_bias, norm_gain, norm_bias)])
    got_outer = across(outer)

    middle, beside = call(
        middle_kernel,
        "middle",
        [array(half, width), array(rows, width)],
        [VMEM] * 3,
        [VMEM] * 2,
        [pltpu.VMEM((half, width), F32)],
    )(x, taps, vectors)
    got_middle = across(middle)

    sides = swap(
        call(
            relay_kernel,
            "relay",
            array(2 * rows, width),
            [VMEM] * 3,
            VMEM,
            [],
        )(beside, got_outer[0], got_outer[-1])
    )

    pair, cross = call(
        ends_kernel,
        "ends",
        [array(cols + 2, width)] * 2,
        [VMEM] * 2,
        [VMEM] * 2,
        [],
    )(x, sides)
    def side(last):
        return call(
            functools.partial(side_kernel, last),
            "side",
            array(half, width),
            [VMEM] * 4,
            VMEM,
            [pltpu.VMEM((rows, width), F32), pltpu.VMEM((half, width), F32)],
        )(x, sides, taps, vectors)

    near, far = [side(0)], [side(1)]
    got_near = [across(v) for v in near]
    got_far = [across(v) for v in far]
    marks = {"A2": got_middle, "B": sum(got_near, []), "C1": got_far[0]}

    def hold(place, values):
        others = sum([marks[k] for k in marks if K[k] == place], [])
        return after(values, others) if others else list(values)

    pair, cross = hold("up", (pair, cross))
    pair, cross = exchange(pair, 0), exchange(cross, 1)
    pair, cross = hold("edges", (pair, cross))
    edge = call(
        edges_kernel,
        "edges",
        array(2 * cols, width),
        [VMEM] * 6,
        VMEM,
        [pltpu.VMEM((2 * cols, width), F32)],
    )(x, sides, pair, cross, taps, vectors)
    got_edge = across(edge)
    marks["D"] = got_edge

    shape = (3, qkv_weight.shape[2] // HD, rows, side_count * cols * HD)
    weight = jnp.swapaxes(qkv_weight, 1, 2)
    run = functools.partial(project, weight=weight, bias=qkv_bias, rows=rows, side_count=side_count, shape=shape)

    def whole(values):
        return [(value, 0, value.shape[0]) for value in values]

    def groups_of(near, middle, edge, far, other):
        return [
            (whole(near) + [(edge, 0, two)], other, 0),
            (whole(middle) + [(edge, two, two)], other, 1),
            (whole(far) + [(edge, 2 * two, two)], other, 2),
        ]

    def step_on(out, groups, step):
        arrays, entries = [], []
        for pieces, other, group in groups:
            entry = []
            for value, at, size in pieces:
                entry.append((len(arrays), at, size))
                arrays.append(value)
            entries.append((tuple(entry), other, group))
        return run(out, arrays, entries, step)

    (late,) = hold("eswap", (edge,))
    (held,) = hold("X", (middle,))
    out = step_on(
        None,
        groups_of(near, [held], edge, far, 0)
        + groups_of([swap(v) for v in near], [swap(middle)], swap(late), [swap(far[0][p : p + K['pieceF']]) for p in range(0, half, K['pieceF'])], 1),
        0,
    )
    for step in steps:
        at = step - 1
        pick = dict(
            swA=[got_middle[at]], swB=[v[at] for v in got_near], swD=[got_edge[at]]
        )
        for key in pick:
            if K[key] == "X":
                *pick[key], out = lax.optimization_barrier((*pick[key], out))
        c1 = [v[at] for v in got_far]
        if K["C1"] == "dswap":
            pick["swD"] = after(pick["swD"], c1[:1])
        gota, gotb, (gote,) = pick["swA"], pick["swB"], pick["swD"]
        other_near = [swap(v[p : p + K["piece"]]) for v in gotb for p in range(0, v.shape[0], K["piece"])]
        other_middle = [swap(v[p : p + K["pieceA"]]) for v in gota for p in range(0, v.shape[0], K["pieceA"])]
        othere = swap(gote)
        mine = groups_of(gotb, gota, gote, [], 0)[:2]
        theirs = groups_of(other_near, other_middle, othere, [], 1)[:2]
        if K["y"] == 2:
            out = step_on(out, mine, chips - step)
            out = step_on(out, theirs, chips - step)
        else:
            out = step_on(out, mine + theirs, chips - step)
        *c1, out = lax.optimization_barrier((*c1, out))
        last = groups_of([], [], gote, c1, 0)[2:]
        other = groups_of([], [], othere, [swap(v) for v in c1], 1)[2:]
        if K["z"] == 2:
            out = step_on(out, last, chips - step)
            out = step_on(out, other, chips - step)
        else:
            out = step_on(out, last + other, chips - step)
    return out


def solution(mesh):
    placed = (P("rows", "cols", None), P(), P(), P(), P(), P(None, None, "cols"), P(None, "cols"))
    return jax.shard_map(
        local, mesh=mesh, in_specs=placed, out_specs=P(None, "cols", "rows", None), check_vma=False
    )
```

```python
import functools

import jax
import jax.numpy as jnp
from jax import lax
from jax.experimental import pallas as pl
from jax.experimental.pallas import tpu as pltpu
from jax.sharding import PartitionSpec as P

HD = 80
GROUP = 8
LANES = 128
EPS = 1e-06
VMEM_LIMIT = 32 * 1024 * 1024
PIECE = 96
OWN_PIECE = 128
LAST_PIECE = 176
BF16 = jnp.bfloat16
F32 = jnp.float32

VMEM = pl.BlockSpec(memory_space=pltpu.VMEM)
HBM = pl.BlockSpec(memory_space=pltpu.HBM)


def call(body, name, outs, specs, out_specs, scratch, aliases=None):
    return pl.pallas_call(
        body,
        out_shape=outs,
        in_specs=specs,
        out_specs=out_specs,
        scratch_shapes=scratch,
        input_output_aliases=aliases or {},
        compiler_params=pltpu.CompilerParams(vmem_limit_bytes=VMEM_LIMIT),
        cost_estimate=pl.CostEstimate(flops=1024, bytes_accessed=1024, transcendentals=0),
        name=name,
    )


def stencil(taps_ref, bias_ref, lanes, cells, first, count, emit):
    taps = [[taps_ref[a, pl.ds(b, 1), lanes] for b in range(3)] for a in range(3)]
    bias = bias_ref[:, lanes]
    above = here = None
    for i in range(first - 1, first + count + 1):
        l, c, r = cells(i)
        part = [taps[a][0] * l + taps[a][1] * c + taps[a][2] * r for a in range(3)]
        if i > first:
            emit(i - 1, above + part[2])
        if i >= first:
            above = here + (part[1] + c)
        here = part[0] + bias


def normalize(mixed, count, gain_ref, nbias_ref, out_ref):
    width = mixed.shape[1]
    tiles = [pl.ds(k, LANES) for k in range(0, width, LANES)]
    total = mixed[:count, tiles[0]]
    for lanes in tiles[1:]:
        total = total + mixed[:count, lanes]
    mean = jnp.sum(total, axis=1, keepdims=True) * (1.0 / width)
    square = None
    for lanes in tiles:
        centered = mixed[:count, lanes] - mean
        square = centered * centered if square is None else square + centered * centered
    scale = lax.rsqrt(jnp.sum(square, axis=1, keepdims=True) * (1.0 / width) + EPS)
    for lanes in tiles:
        value = (mixed[:count, lanes] - mean) * scale * gain_ref[:, lanes] + nbias_ref[:, lanes]
        out_ref[:count, lanes] = value.astype(BF16)


def each_tile(width, body):
    def step(k, _):
        body(pl.ds(pl.multiple_of(k * LANES, LANES), LANES))
        return 0

    lax.fori_loop(0, width // LANES, step, 0)


def middle_cells(x_ref, lanes, span):
    cols = x_ref.shape[1]

    def cells(i):
        x = x_ref[i, :, lanes].astype(F32)
        return pltpu.roll(x, 1, 0)[span], x[span], pltpu.roll(x, cols - 1, 0)[span]

    return cells


def core_of(cols_axis):
    return lax.rem(lax.axis_index(cols_axis), 2)


def column(x_ref, first, count, last, lanes):
    cols = x_ref.shape[1]
    part = pl.multiple_of(jnp.where(last, cols - GROUP, 0), GROUP)
    cells = [x_ref[i, pl.ds(part, GROUP), lanes].astype(F32) for i in range(first, first + count)]
    cells = [jnp.where(last, cell[GROUP - 1 :], cell[:1]) for cell in cells]
    return jnp.concatenate(cells, axis=0).astype(BF16)


def first_kernel(x_hbm, taps_hbm, cbias_hbm, gain_hbm, nbias_hbm, outer_ref, x_ref, taps_ref, vec_ref, *rest):
    *flat, sems = rest
    rows, _, width = x_ref.shape
    spans = [pl.ds(at, GROUP) for at in range(0, rows, GROUP)]
    pairs = [(x_hbm.at[span], x_ref.at[span]) for span in spans]
    pairs += [(taps_hbm, taps_ref), (cbias_hbm, flat[0]), (gain_hbm, flat[1]), (nbias_hbm, flat[2])]
    copies = [pltpu.make_async_copy(source, target, sems.at[k]) for k, (source, target) in enumerate(pairs)]
    for copy in copies:
        copy.start()
    last = core_of("cols") == 1
    for k, span in enumerate(spans):
        copies[k].wait()
        for at in range(0, width, LANES):
            lanes = pl.ds(at, LANES)
            outer_ref[span, lanes] = column(x_ref, k * GROUP, GROUP, last, lanes)
    for copy in copies[len(spans) :]:
        copy.wait()
    for k, ref in enumerate(flat):
        vec_ref[k] = ref[...].reshape(1, width)


def middle_kernel(x_ref, taps_ref, vec_ref, out_ref, inner_ref, mixed):
    rows, cols, width = x_ref.shape
    start = 1
    span = slice(GROUP, cols - GROUP)
    wide = cols - 2 * GROUP
    count = rows - 1 - start

    def tile(lanes):
        def emit(i, value):
            mixed[pl.ds((i - start) * wide, wide), lanes] = value

        stencil(taps_ref, vec_ref.at[0], lanes, middle_cells(x_ref, lanes, span), start, count, emit)
        inner_ref[:, lanes] = column(x_ref, 0, rows, core_of("cols") == 0, lanes)

    each_tile(width, tile)
    normalize(mixed, count * wide, vec_ref.at[1], vec_ref.at[2], out_ref)


def relay_kernel(beside_ref, before_ref, behind_ref, out_ref):
    rows = beside_ref.shape[0]
    col, count = lax.axis_index("cols"), lax.axis_size("cols")
    core = core_of("cols")
    none = jnp.logical_or(col == 1, col == count - 2)
    out_ref[:rows, :] = beside_ref[...]
    passed = jnp.where(core == 1, before_ref[...].astype(F32), behind_ref[...].astype(F32))
    out_ref[rows:, :] = jnp.where(none, 0.0, passed).astype(BF16)


def halves(sides_ref, rows, lanes):
    other, passed = sides_ref[:rows, lanes].astype(F32), sides_ref[rows:, lanes].astype(F32)
    core = core_of("cols")
    return jnp.where(core == 1, other, passed), jnp.where(core == 1, passed, other)


def ends_kernel(x_ref, sides_ref, pair_ref, cross_ref):
    rows, cols, _ = x_ref.shape
    lefts, rights = halves(sides_ref, rows, slice(None))
    odd = lax.rem(lax.axis_index("rows"), 2) == 1

    for ref, at in ((pair_ref, (0, rows - 1)), (cross_ref, (rows - 1, 0))):
        ref[:cols, :] = jnp.where(odd, x_ref[at[0]].astype(F32), x_ref[at[1]].astype(F32)).astype(BF16)
        ends = [
            jnp.where(odd, column[at[0] : at[0] + 1], column[at[1] : at[1] + 1]) for column in (lefts, rights)
        ]
        ref[cols:, :] = jnp.concatenate(ends, axis=0).astype(BF16)


def side_kernel(last, x_ref, sides_ref, taps_ref, vec_ref, out_ref, beside, mixed):
    rows, cols, width = x_ref.shape
    place = lax.broadcasted_iota(jnp.int32, (GROUP, LANES), 0)
    beside[...] = halves(sides_ref, rows, slice(None))[last]

    def tile(lanes):
        def cells(i):
            x = x_ref[i, :, lanes].astype(F32)
            edge = beside[pl.ds(i, 1), lanes]
            if last:
                here, both = x[cols - GROUP :], x[cols - 2 * GROUP :]
                r = jnp.where(place == GROUP - 1, edge, pltpu.roll(here, GROUP - 1, 0))
                return pltpu.roll(both, 1, 0)[GROUP:], here, r
            here, both = x[:GROUP], x[: 2 * GROUP]
            l = jnp.where(place == 0, edge, pltpu.roll(here, 1, 0))
            return l, here, pltpu.roll(both, 2 * GROUP - 1, 0)[:GROUP]

        def emit(i, value):
            mixed[pl.ds((i - 1) * GROUP, GROUP), lanes] = value

        stencil(taps_ref, vec_ref.at[0], lanes, cells, 1, rows - 2, emit)

    each_tile(width, tile)
    normalize(mixed, mixed.shape[0], vec_ref.at[1], vec_ref.at[2], out_ref)


def edges_kernel(x_ref, sides_ref, pair_ref, cross_ref, taps_ref, vec_ref, out_ref, mixed):
    rows, cols, width = x_ref.shape
    place = lax.broadcasted_iota(jnp.int32, (cols, LANES), 0)
    odd = lax.rem(lax.axis_index("rows"), 2) == 1

    def tile(lanes):
        lefts, rights = halves(sides_ref, rows, lanes)
        pair, cross = pair_ref[:, lanes].astype(F32), cross_ref[:, lanes].astype(F32)
        up, down = jnp.where(odd, pair, cross), jnp.where(odd, cross, pair)

        def cells(i):
            if i < 0:
                x, l, r = up[:cols], up[cols : cols + 1], up[cols + 1 :]
            elif i == rows:
                x, l, r = down[:cols], down[cols : cols + 1], down[cols + 1 :]
            else:
                x, l, r = x_ref[i, :, lanes].astype(F32), lefts[i : i + 1], rights[i : i + 1]
            return (
                jnp.where(place == 0, l, pltpu.roll(x, 1, 0)),
                x,
                jnp.where(place == cols - 1, r, pltpu.roll(x, cols - 1, 0)),
            )

        def emit(i, value):
            for g in range(cols // GROUP):
                at = 2 * g * GROUP + (GROUP if i else 0)
                mixed[pl.ds(at, GROUP), lanes] = value[g * GROUP : (g + 1) * GROUP]

        stencil(taps_ref, vec_ref.at[0], lanes, cells, 0, 1, emit)
        stencil(taps_ref, vec_ref.at[0], lanes, cells, rows - 1, 1, emit)

    each_tile(width, tile)
    normalize(mixed, 2 * cols, vec_ref.at[1], vec_ref.at[2], out_ref)


def project_kernel(rows, plan, count, mode, step, side_count, *refs):
    parts, (w_ref, b_ref), refs = refs[:count], refs[count : count + 2], refs[count + 2 :]
    if mode == "blocks":
        blocks, sums = refs
    else:
        if mode == "last":
            before, refs = refs[0], refs[1:]
        if mode != "first":
            refs = refs[1:]
        out_ref, sums, blocks, sems = refs
    heads = w_ref.shape[1] // HD
    width = w_ref.shape[2]
    total = 3 * heads * HD
    block = GROUP * HD
    weight = w_ref[...].reshape(total, width)
    bias = jnp.concatenate([b_ref[pl.ds(t, 1), :].astype(F32) for t in range(3)], axis=1)
    owner = lax.rem(lax.axis_index("cols") + 2 * step, side_count)
    side = rows * GROUP
    copies = []

    def write(source, other, group, t, sem):
        position = owner ^ 1 if other else owner
        lane = pl.multiple_of(position * (out_ref.shape[3] // side_count) + group * block, LANES)
        copies.append(pltpu.make_async_copy(source.at[t], out_ref.at[t, :, :, pl.ds(lane, block)], sem))
        copies[-1].start()

    if mode == "last":
        for g, (_, other, group) in enumerate(plan):
            for t in range(3):
                write(before.at[g], 1 - other, group, t, sems.at[len(plan) + g, t])
    for batch in batches_of(len(plan)):
        pieces = [parts[ref][pl.ds(at, size), :] for g in batch for ref, at, size in plan[g][0]]
        acc = (
            lax.dot_general(
                jnp.concatenate(pieces, axis=0), weight, (((1,), (1,)), ((), ())), preferred_element_type=F32
            )
            + bias
        )
        inner = side - 2 * GROUP
        for n, g in enumerate(batch):
            for k in range(0, total, LANES):
                piece = acc[n * side : (n + 1) * side, k : k + LANES]
                span = pl.ds(0, piece.shape[1])
                sums[g, k // LANES, pl.ds(GROUP, inner), span] = piece[:inner]
                sums[g, k // LANES, pl.ds(0, GROUP), span] = piece[inner : inner + GROUP]
                sums[g, k // LANES, pl.ds(inner + GROUP, GROUP), span] = piece[inner + GROUP :]
    for g, (_, other, group) in enumerate(plan):
        for t in range(3):
            for h in range(heads):
                start = (t * heads + h) * HD
                lo, hi = start // LANES, (start + HD - 1) // LANES + 1
                cells = []
                for j in range(GROUP):
                    tiles = [sums[g, k, pl.ds(j, rows, stride=GROUP), :] for k in range(lo, hi)]
                    cell = tiles[0] if len(tiles) == 1 else jnp.concatenate(tiles, axis=1)
                    cells.append(cell[:, start - lo * LANES : start - lo * LANES + HD])
                blocks[g, t, h] = jnp.concatenate(cells, axis=1).astype(BF16)
            if mode != "blocks":
                write(blocks.at[g], other, group, t, sems.at[g, t])
    for copy in copies:
        copy.wait()


def batches_of(count):
    size = 3 if count % 3 == 0 else 2
    return [range(at, min(at + size, count)) for at in range(0, count, size)]


def project(out, parts, plan, step, weight, bias, rows, side_count, shape, mode, before=None):
    count = len(parts)
    heads = weight.shape[1] // HD
    operands = [*parts, weight, bias] + [v for v in (before, out) if v is not None]
    sums = pltpu.VMEM((len(plan), pl.cdiv(3 * heads * HD, LANES), (rows + 1) * GROUP, LANES), F32)
    blocks = (len(plan), 3, heads, rows, GROUP * HD)
    body = functools.partial(project_kernel, rows, plan, count, mode, step, side_count)
    specs = [VMEM] * (count + 2 + (before is not None)) + [HBM] * (out is not None)
    if mode == "blocks":
        return call(body, "project", jax.ShapeDtypeStruct(blocks, BF16), specs, VMEM, [sums])(*operands)
    return call(
        body,
        "project",
        jax.ShapeDtypeStruct(shape, BF16),
        specs,
        HBM,
        [sums, pltpu.VMEM(blocks, BF16), pltpu.SemaphoreType.DMA(((2 if mode == "last" else 1) * len(plan), 3))],
        aliases={} if out is None else {len(operands) - 1: 0},
    )(*operands)


def local(patches, conv_taps, conv_bias, norm_gain, norm_bias, qkv_weight, qkv_bias):
    rows, cols, width = patches.shape
    up_count, side_count = lax.axis_size("rows"), lax.axis_size("cols")
    chips = side_count // 2
    inner = rows - 2
    half = inner * GROUP
    two = 2 * GROUP
    steps = range(1, chips)

    def array(*shape, dtype=BF16):
        return jax.ShapeDtypeStruct(shape, dtype)

    def across(value):
        return [
            lax.ppermute(value, "cols", [(q, (q + 2 * step) % side_count) for q in range(side_count)])
            for step in steps
        ]

    def swap(value):
        return lax.ppermute(value, "cols", [(q, q ^ 1) for q in range(side_count)])

    def exchange(value, start):
        pairs = [(i, i + 1) for i in range(start, up_count - 1, 2)]
        return lax.ppermute(value, "rows", pairs + [(j, i) for i, j in pairs])

    def after(values, others):
        joined = lax.optimization_barrier((*values, *others))
        return list(joined[: len(values)])

    def in_hbm(value):
        return pltpu.with_memory_space_constraint(value, pltpu.HBM)

    outer, x, taps, vectors = call(
        first_kernel,
        "first",
        [
            array(rows, width),
            array(rows, cols, width),
            array(3, 3, width, dtype=F32),
            array(3, 1, width, dtype=F32),
        ],
        [HBM] * 5,
        [VMEM] * 4,
        [pltpu.VMEM((width,), F32)] * 3 + [pltpu.SemaphoreType.DMA((rows // GROUP + 4,))],
    )(*[in_hbm(v) for v in (patches, conv_taps, conv_bias, norm_gain, norm_bias)])
    got_outer = across(outer)

    middle, beside = call(
        middle_kernel,
        "middle",
        [array(half, width), array(rows, width)],
        [VMEM] * 3,
        [VMEM] * 2,
        [pltpu.VMEM((half, width), F32)],
    )(x, taps, vectors)
    got_middle = across(middle)

    sides = swap(
        call(
            relay_kernel,
            "relay",
            array(2 * rows, width),
            [VMEM] * 3,
            VMEM,
            [],
        )(beside, got_outer[0], got_outer[-1])
    )

    pair, cross = call(
        ends_kernel,
        "ends",
        [array(cols + 2, width)] * 2,
        [VMEM] * 2,
        [VMEM] * 2,
        [],
    )(x, sides)

    def side(last):
        return call(
            functools.partial(side_kernel, last),
            "side",
            array(half, width),
            [VMEM] * 4,
            VMEM,
            [pltpu.VMEM((rows, width), F32), pltpu.VMEM((half, width), F32)],
        )(x, sides, taps, vectors)

    near, far = side(0), side(1)
    got_near, got_far = across(near), across(far)
    pair, cross = after((exchange(pair, 0), exchange(cross, 1)), got_middle)
    edge = call(
        edges_kernel,
        "edges",
        array(2 * cols, width),
        [VMEM] * 6,
        VMEM,
        [pltpu.VMEM((2 * cols, width), F32)],
    )(x, sides, pair, cross, taps, vectors)
    got_edge = across(edge)

    shape = (3, qkv_weight.shape[2] // HD, rows, side_count * cols * HD)
    weight = jnp.swapaxes(qkv_weight, 1, 2)
    run = functools.partial(project, weight=weight, bias=qkv_bias, rows=rows, side_count=side_count, shape=shape)

    def whole(values):
        return [(value, 0, value.shape[0]) for value in values]

    def groups_of(near, middle, edge, far, other):
        return [
            (whole(near) + [(edge, 0, two)], other, 0),
            (whole(middle) + [(edge, two, two)], other, 1),
            (whole(far) + [(edge, 2 * two, two)], other, 2),
        ]

    def step_on(out, groups, step, mode="next", before=None):
        arrays, entries = [], []
        for pieces, other, group in groups:
            entry = []
            for value, at, size in pieces:
                entry.append((len(arrays), at, size))
                arrays.append(value)
            entries.append((tuple(entry), other, group))
        return run(out, arrays, entries, step, mode=mode, before=before)

    def cut(value, size):
        return [value[at : at + size] for at in range(0, value.shape[0], size)]

    def swaps(value, size=half):
        return [swap(part) for part in cut(value, size)]

    own = groups_of([near], [middle], edge, [far], 0)
    own = own + groups_of(swaps(near), swaps(middle), swap(edge), swaps(far, OWN_PIECE), 1)
    out = step_on(None, own, 0, "first")
    for step in steps:
        got = [v[step - 1] for v in (got_near, got_middle, got_edge)]
        *got, out = lax.optimization_barrier((*got, out))
        one, second, border = got
        other_border = swap(border)
        out = step_on(out, groups_of([one], [second], border, [], 0)[:2], chips - step)
        theirs = groups_of(swaps(one, PIECE), swaps(second, PIECE), other_border, [], 1)[:2]
        out = step_on(out, theirs, chips - step)
        last, out = lax.optimization_barrier((got_far[step - 1], out))
        blocks = step_on(None, groups_of([], [], border, [last], 0)[2:], chips - step, "blocks")
        theirs = groups_of([], [], other_border, swaps(last, LAST_PIECE), 1)[2:]
        out = step_on(out, theirs, chips - step, "last", blocks)
    return out


def solution(mesh):
    placed = (P("rows", "cols", None), P(), P(), P(), P(), P(None, None, "cols"), P(None, "cols"))
    return jax.shard_map(
        local, mesh=mesh, in_specs=placed, out_specs=P(None, "cols", "rows", None), check_vma=False
    )
```

```python
import functools

import jax
import jax.numpy as jnp
from jax import lax
from jax.experimental import pallas as pl
from jax.experimental.pallas import tpu as pltpu
from jax.sharding import PartitionSpec as P

HD = 80
GROUP = 8
LANES = 128
EPS = 1e-06
VMEM_LIMIT = 32 * 1024 * 1024
PIECE = 96
OWN_PIECE = 128
LAST_PIECE = 176
BF16 = jnp.bfloat16
F32 = jnp.float32

VMEM = pl.BlockSpec(memory_space=pltpu.VMEM)
HBM = pl.BlockSpec(memory_space=pltpu.HBM)


def call(body, name, outs, specs, out_specs, scratch, aliases=None):
    return pl.pallas_call(
        body,
        out_shape=outs,
        in_specs=specs,
        out_specs=out_specs,
        scratch_shapes=scratch,
        input_output_aliases=aliases or {},
        compiler_params=pltpu.CompilerParams(vmem_limit_bytes=VMEM_LIMIT),
        cost_estimate=pl.CostEstimate(flops=1024, bytes_accessed=1024, transcendentals=0),
        name=name,
    )


def stencil(taps_ref, bias_ref, lanes, cells, first, count, emit):
    taps = [[taps_ref[a, pl.ds(b, 1), lanes] for b in range(3)] for a in range(3)]
    bias = bias_ref[:, lanes]
    above = here = None
    for i in range(first - 1, first + count + 1):
        l, c, r = cells(i)
        part = [taps[a][0] * l + taps[a][1] * c + taps[a][2] * r for a in range(3)]
        if i > first:
            emit(i - 1, above + part[2])
        if i >= first:
            above = here + (part[1] + c)
        here = part[0] + bias


def normalize(mixed, count, gain_ref, nbias_ref, out_ref):
    width = mixed.shape[1]
    tiles = [pl.ds(k, LANES) for k in range(0, width, LANES)]
    total = mixed[:count, tiles[0]]
    for lanes in tiles[1:]:
        total = total + mixed[:count, lanes]
    mean = jnp.sum(total, axis=1, keepdims=True) * (1.0 / width)
    square = None
    for lanes in tiles:
        centered = mixed[:count, lanes] - mean
        square = centered * centered if square is None else square + centered * centered
    scale = lax.rsqrt(jnp.sum(square, axis=1, keepdims=True) * (1.0 / width) + EPS)
    for lanes in tiles:
        value = (mixed[:count, lanes] - mean) * scale * gain_ref[:, lanes] + nbias_ref[:, lanes]
        out_ref[:count, lanes] = value.astype(BF16)


def each_tile(width, body):
    def step(k, _):
        body(pl.ds(pl.multiple_of(k * LANES, LANES), LANES))
        return 0

    lax.fori_loop(0, width // LANES, step, 0)


def middle_cells(x_ref, lanes, span):
    cols = x_ref.shape[1]

    def cells(i):
        x = x_ref[i, :, lanes].astype(F32)
        return pltpu.roll(x, 1, 0)[span], x[span], pltpu.roll(x, cols - 1, 0)[span]

    return cells


def core_of(cols_axis):
    return lax.rem(lax.axis_index(cols_axis), 2)


def column(x_ref, first, count, last, lanes):
    cols = x_ref.shape[1]
    part = pl.multiple_of(jnp.where(last, cols - GROUP, 0), GROUP)
    cells = [x_ref[i, pl.ds(part, GROUP), lanes].astype(F32) for i in range(first, first + count)]
    cells = [jnp.where(last, cell[GROUP - 1 :], cell[:1]) for cell in cells]
    return jnp.concatenate(cells, axis=0).astype(BF16)


def first_kernel(x_hbm, taps_hbm, cbias_hbm, gain_hbm, nbias_hbm, outer_ref, x_ref, taps_ref, vec_ref, *rest):
    *flat, sems = rest
    rows, _, width = x_ref.shape
    spans = [pl.ds(at, GROUP) for at in range(0, rows, GROUP)]
    pairs = [(x_hbm.at[span], x_ref.at[span]) for span in spans]
    pairs += [(taps_hbm, taps_ref), (cbias_hbm, flat[0]), (gain_hbm, flat[1]), (nbias_hbm, flat[2])]
    copies = [pltpu.make_async_copy(source, target, sems.at[k]) for k, (source, target) in enumerate(pairs)]
    for copy in copies:
        copy.start()
    last = core_of("cols") == 1
    for k, span in enumerate(spans):
        copies[k].wait()
        for at in range(0, width, LANES):
            lanes = pl.ds(at, LANES)
            outer_ref[span, lanes] = column(x_ref, k * GROUP, GROUP, last, lanes)
    for copy in copies[len(spans) :]:
        copy.wait()
    for k, ref in enumerate(flat):
        vec_ref[k] = ref[...].reshape(1, width)


def middle_kernel(x_ref, taps_ref, vec_ref, out_ref, inner_ref, mixed):
    rows, cols, width = x_ref.shape
    start = 1
    span = slice(GROUP, cols - GROUP)
    wide = cols - 2 * GROUP
    count = rows - 1 - start

    def tile(lanes):
        def emit(i, value):
            mixed[pl.ds((i - start) * wide, wide), lanes] = value

        stencil(taps_ref, vec_ref.at[0], lanes, middle_cells(x_ref, lanes, span), start, count, emit)
        inner_ref[:, lanes] = column(x_ref, 0, rows, core_of("cols") == 0, lanes)

    each_tile(width, tile)
    normalize(mixed, count * wide, vec_ref.at[1], vec_ref.at[2], out_ref)


def relay_kernel(beside_ref, before_ref, behind_ref, out_ref):
    rows = beside_ref.shape[0]
    col, count = lax.axis_index("cols"), lax.axis_size("cols")
    core = core_of("cols")
    none = jnp.logical_or(col == 1, col == count - 2)
    out_ref[:rows, :] = beside_ref[...]
    passed = jnp.where(core == 1, before_ref[...].astype(F32), behind_ref[...].astype(F32))
    out_ref[rows:, :] = jnp.where(none, 0.0, passed).astype(BF16)


def halves(sides_ref, rows, lanes):
    other, passed = sides_ref[:rows, lanes].astype(F32), sides_ref[rows:, lanes].astype(F32)
    core = core_of("cols")
    return jnp.where(core == 1, other, passed), jnp.where(core == 1, passed, other)


def ends_kernel(x_ref, sides_ref, pair_ref, cross_ref):
    rows, cols, _ = x_ref.shape
    lefts, rights = halves(sides_ref, rows, slice(None))
    odd = lax.rem(lax.axis_index("rows"), 2) == 1

    for ref, at in ((pair_ref, (0, rows - 1)), (cross_ref, (rows - 1, 0))):
        ref[:cols, :] = jnp.where(odd, x_ref[at[0]].astype(F32), x_ref[at[1]].astype(F32)).astype(BF16)
        ends = [
            jnp.where(odd, column[at[0] : at[0] + 1], column[at[1] : at[1] + 1]) for column in (lefts, rights)
        ]
        ref[cols:, :] = jnp.concatenate(ends, axis=0).astype(BF16)


def side_kernel(last, x_ref, sides_ref, taps_ref, vec_ref, out_ref, beside, mixed):
    rows, cols, width = x_ref.shape
    place = lax.broadcasted_iota(jnp.int32, (GROUP, LANES), 0)
    beside[...] = halves(sides_ref, rows, slice(None))[last]

    def tile(lanes):
        def cells(i):
            x = x_ref[i, :, lanes].astype(F32)
            edge = beside[pl.ds(i, 1), lanes]
            if last:
                here, both = x[cols - GROUP :], x[cols - 2 * GROUP :]
                r = jnp.where(place == GROUP - 1, edge, pltpu.roll(here, GROUP - 1, 0))
                return pltpu.roll(both, 1, 0)[GROUP:], here, r
            here, both = x[:GROUP], x[: 2 * GROUP]
            l = jnp.where(place == 0, edge, pltpu.roll(here, 1, 0))
            return l, here, pltpu.roll(both, 2 * GROUP - 1, 0)[:GROUP]

        def emit(i, value):
            mixed[pl.ds((i - 1) * GROUP, GROUP), lanes] = value

        stencil(taps_ref, vec_ref.at[0], lanes, cells, 1, rows - 2, emit)

    each_tile(width, tile)
    normalize(mixed, mixed.shape[0], vec_ref.at[1], vec_ref.at[2], out_ref)


def edges_kernel(x_ref, sides_ref, pair_ref, cross_ref, taps_ref, vec_ref, out_ref, mixed):
    rows, cols, width = x_ref.shape
    place = lax.broadcasted_iota(jnp.int32, (cols, LANES), 0)
    odd = lax.rem(lax.axis_index("rows"), 2) == 1

    def tile(lanes):
        lefts, rights = halves(sides_ref, rows, lanes)
        pair, cross = pair_ref[:, lanes].astype(F32), cross_ref[:, lanes].astype(F32)
        up, down = jnp.where(odd, pair, cross), jnp.where(odd, cross, pair)

        def cells(i):
            if i < 0:
                x, l, r = up[:cols], up[cols : cols + 1], up[cols + 1 :]
            elif i == rows:
                x, l, r = down[:cols], down[cols : cols + 1], down[cols + 1 :]
            else:
                x, l, r = x_ref[i, :, lanes].astype(F32), lefts[i : i + 1], rights[i : i + 1]
            return (
                jnp.where(place == 0, l, pltpu.roll(x, 1, 0)),
                x,
                jnp.where(place == cols - 1, r, pltpu.roll(x, cols - 1, 0)),
            )

        def emit(i, value):
            for g in range(cols // GROUP):
                at = 2 * g * GROUP + (GROUP if i else 0)
                mixed[pl.ds(at, GROUP), lanes] = value[g * GROUP : (g + 1) * GROUP]

        stencil(taps_ref, vec_ref.at[0], lanes, cells, 0, 1, emit)
        stencil(taps_ref, vec_ref.at[0], lanes, cells, rows - 1, 1, emit)

    each_tile(width, tile)
    normalize(mixed, 2 * cols, vec_ref.at[1], vec_ref.at[2], out_ref)


def project_kernel(rows, plan, count, mode, step, side_count, *refs):
    parts, (w_ref, b_ref), refs = refs[:count], refs[count : count + 2], refs[count + 2 :]
    if mode == "blocks":
        blocks, sums = refs
    else:
        if mode == "last":
            before, refs = refs[0], refs[1:]
        if mode != "first":
            refs = refs[1:]
        out_ref, sums, blocks, sems = refs
    heads = w_ref.shape[1] // HD
    width = w_ref.shape[2]
    total = 3 * heads * HD
    block = GROUP * HD
    weight = w_ref[...].reshape(total, width)
    bias = jnp.concatenate([b_ref[pl.ds(t, 1), :].astype(F32) for t in range(3)], axis=1)
    owner = lax.rem(lax.axis_index("cols") + 2 * step, side_count)
    side = rows * GROUP
    copies = []

    def write(source, other, group, t, sem):
        position = owner ^ 1 if other else owner
        lane = pl.multiple_of(position * (out_ref.shape[3] // side_count) + group * block, LANES)
        copies.append(pltpu.make_async_copy(source.at[t], out_ref.at[t, :, :, pl.ds(lane, block)], sem))
        copies[-1].start()

    if mode == "last":
        for g, (_, other, group) in enumerate(plan):
            for t in range(3):
                write(before.at[g], 1 - other, group, t, sems.at[len(plan) + g, t])
    inner = side - 2 * GROUP

    def multiply(batch, lo, hi):
        pieces = [parts[ref][pl.ds(at, size), :] for g in batch for ref, at, size in plan[g][0]]
        acc = lax.dot_general(
            jnp.concatenate(pieces, axis=0), weight[lo:hi], (((1,), (1,)), ((), ())), preferred_element_type=F32
        )
        acc = acc + bias[:, lo:hi]
        for n, g in enumerate(batch):
            for k in range(lo, hi, LANES):
                piece = acc[n * side : (n + 1) * side, k - lo : min(k + LANES, hi) - lo]
                span = pl.ds(0, piece.shape[1])
                sums[g, k // LANES, pl.ds(GROUP, inner), span] = piece[:inner]
                sums[g, k // LANES, pl.ds(0, GROUP), span] = piece[inner : inner + GROUP]
                sums[g, k // LANES, pl.ds(inner + GROUP, GROUP), span] = piece[inner + GROUP :]

    def lay_out(g, t):
        for h in range(heads):
            start = (t * heads + h) * HD
            lo, hi = start // LANES, (start + HD - 1) // LANES + 1
            cells = []
            for j in range(GROUP):
                tiles = [sums[g, k, pl.ds(j, rows, stride=GROUP), :] for k in range(lo, hi)]
                cell = tiles[0] if len(tiles) == 1 else jnp.concatenate(tiles, axis=1)
                cells.append(cell[:, start - lo * LANES : start - lo * LANES + HD])
            blocks[g, t, h] = jnp.concatenate(cells, axis=1).astype(BF16)
        if mode != "blocks":
            write(blocks.at[g], plan[g][1], plan[g][2], t, sems.at[g, t])

    half = min(4 * LANES, total) if len(plan) == 1 else total
    ready = 0
    for lo, hi in ((0, half), (half, total)):
        if lo < hi:
            for batch in batches_of(len(plan)):
                multiply(batch, lo, hi)
        complete = hi // (heads * HD)
        for g in range(len(plan)):
            for t in range(ready, complete):
                lay_out(g, t)
        ready = complete
    for copy in copies:
        copy.wait()


def batches_of(count):
    size = 3 if count % 3 == 0 else 2
    return [range(at, min(at + size, count)) for at in range(0, count, size)]


def project(out, parts, plan, step, weight, bias, rows, side_count, shape, mode, before=None):
    count = len(parts)
    heads = weight.shape[1] // HD
    operands = [*parts, weight, bias] + [v for v in (before, out) if v is not None]
    sums = pltpu.VMEM((len(plan), pl.cdiv(3 * heads * HD, LANES), (rows + 1) * GROUP, LANES), F32)
    blocks = (len(plan), 3, heads, rows, GROUP * HD)
    body = functools.partial(project_kernel, rows, plan, count, mode, step, side_count)
    specs = [VMEM] * (count + 2 + (before is not None)) + [HBM] * (out is not None)
    if mode == "blocks":
        return call(body, "project", jax.ShapeDtypeStruct(blocks, BF16), specs, VMEM, [sums])(*operands)
    return call(
        body,
        "project",
        jax.ShapeDtypeStruct(shape, BF16),
        specs,
        HBM,
        [sums, pltpu.VMEM(blocks, BF16), pltpu.SemaphoreType.DMA(((2 if mode == "last" else 1) * len(plan), 3))],
        aliases={} if out is None else {len(operands) - 1: 0},
    )(*operands)


def local(patches, conv_taps, conv_bias, norm_gain, norm_bias, qkv_weight, qkv_bias):
    rows, cols, width = patches.shape
    up_count, side_count = lax.axis_size("rows"), lax.axis_size("cols")
    chips = side_count // 2
    inner = rows - 2
    half = inner * GROUP
    two = 2 * GROUP
    steps = range(1, chips)

    def array(*shape, dtype=BF16):
        return jax.ShapeDtypeStruct(shape, dtype)

    def across(value):
        return [
            lax.ppermute(value, "cols", [(q, (q + 2 * step) % side_count) for q in range(side_count)])
            for step in steps
        ]

    def swap(value):
        return lax.ppermute(value, "cols", [(q, q ^ 1) for q in range(side_count)])

    def exchange(value, start):
        pairs = [(i, i + 1) for i in range(start, up_count - 1, 2)]
        return lax.ppermute(value, "rows", pairs + [(j, i) for i, j in pairs])

    def after(values, others):
        joined = lax.optimization_barrier((*values, *others))
        return list(joined[: len(values)])

    def in_hbm(value):
        return pltpu.with_memory_space_constraint(value, pltpu.HBM)

    outer, x, taps, vectors = call(
        first_kernel,
        "first",
        [
            array(rows, width),
            array(rows, cols, width),
            array(3, 3, width, dtype=F32),
            array(3, 1, width, dtype=F32),
        ],
        [HBM] * 5,
        [VMEM] * 4,
        [pltpu.VMEM((width,), F32)] * 3 + [pltpu.SemaphoreType.DMA((rows // GROUP + 4,))],
    )(*[in_hbm(v) for v in (patches, conv_taps, conv_bias, norm_gain, norm_bias)])
    got_outer = across(outer)

    middle, beside = call(
        middle_kernel,
        "middle",
        [array(half, width), array(rows, width)],
        [VMEM] * 3,
        [VMEM] * 2,
        [pltpu.VMEM((half, width), F32)],
    )(x, taps, vectors)
    got_middle = across(middle)

    sides = swap(
        call(
            relay_kernel,
            "relay",
            array(2 * rows, width),
            [VMEM] * 3,
            VMEM,
            [],
        )(beside, got_outer[0], got_outer[-1])
    )

    pair, cross = call(
        ends_kernel,
        "ends",
        [array(cols + 2, width)] * 2,
        [VMEM] * 2,
        [VMEM] * 2,
        [],
    )(x, sides)

    def side(last):
        return call(
            functools.partial(side_kernel, last),
            "side",
            array(half, width),
            [VMEM] * 4,
            VMEM,
            [pltpu.VMEM((rows, width), F32), pltpu.VMEM((half, width), F32)],
        )(x, sides, taps, vectors)

    near, far = side(0), side(1)
    got_near, got_far = across(near), across(far)
    pair, cross = after((exchange(pair, 0), exchange(cross, 1)), got_middle)
    edge = call(
        edges_kernel,
        "edges",
        array(2 * cols, width),
        [VMEM] * 6,
        VMEM,
        [pltpu.VMEM((2 * cols, width), F32)],
    )(x, sides, pair, cross, taps, vectors)
    got_edge = across(edge)

    shape = (3, qkv_weight.shape[2] // HD, rows, side_count * cols * HD)
    weight = jnp.swapaxes(qkv_weight, 1, 2)
    run = functools.partial(project, weight=weight, bias=qkv_bias, rows=rows, side_count=side_count, shape=shape)

    def whole(values):
        return [(value, 0, value.shape[0]) for value in values]

    def groups_of(near, middle, edge, far, other):
        return [
            (whole(near) + [(edge, 0, two)], other, 0),
            (whole(middle) + [(edge, two, two)], other, 1),
            (whole(far) + [(edge, 2 * two, two)], other, 2),
        ]

    def step_on(out, groups, step, mode="next", before=None):
        arrays, entries = [], []
        for pieces, other, group in groups:
            entry = []
            for value, at, size in pieces:
                entry.append((len(arrays), at, size))
                arrays.append(value)
            entries.append((tuple(entry), other, group))
        return run(out, arrays, entries, step, mode=mode, before=before)

    def cut(value, size):
        return [value[at : at + size] for at in range(0, value.shape[0], size)]

    def swaps(value, size=half):
        return [swap(part) for part in cut(value, size)]

    own = groups_of([near], [middle], edge, [far], 0)
    own = own + groups_of(swaps(near), swaps(middle), swap(edge), swaps(far, OWN_PIECE), 1)
    out = step_on(None, own, 0, "first")
    for step in steps:
        got = [v[step - 1] for v in (got_near, got_middle, got_edge)]
        *got, out = lax.optimization_barrier((*got, out))
        one, second, border = got
        other_border = swap(border)
        out = step_on(out, groups_of([one], [second], border, [], 0)[:2], chips - step)
        theirs = groups_of(swaps(one, PIECE), swaps(second, PIECE), other_border, [], 1)[:2]
        out = step_on(out, theirs, chips - step)
        last, out = lax.optimization_barrier((got_far[step - 1], out))
        blocks = step_on(None, groups_of([], [], border, [last], 0)[2:], chips - step, "blocks")
        theirs = groups_of([], [], other_border, swaps(last, LAST_PIECE), 1)[2:]
        out = step_on(out, theirs, chips - step, "last", blocks)
    return out


def solution(mesh):
    placed = (P("rows", "cols", None), P(), P(), P(), P(), P(None, None, "cols"), P(None, "cols"))
    return jax.shard_map(
        local, mesh=mesh, in_specs=placed, out_specs=P(None, "cols", "rows", None), check_vma=False
    )
```
